32 devices in a mesh: groups: 2 (over x), pairs: 16 (over z, y, core).
Axes of the slice: x: 2, y: 2, z: 4, core: 2. Of those that a mesh axis runs over, the one named last changes fastest.
Arguments:
- amplitudes: float32 [128, 8, 9216], P(('groups', 'pairs')), parts along dimension 0, may hold values from -6 to 6
- block_list: int32 [128, 8], P(('groups', 'pairs')), parts along dimension 0, may hold values from -1 to 63, as said below
- factors: float32 [512, 9216], P(('groups', 'pairs')), parts along dimension 0, may hold values from -0.26 to 0.26
Outputs:
- ladder: float32 [128, 8, 9216], P(('groups', 'pairs')), parts along dimension 0
The draws below stay inside these ranges and needn't reach their ends.
There are 2 independent parts, one for each index of `groups`. The reference program is written for one: setup_inputs(seed, part) draws one part's arguments, and reference() takes and returns one part's arrays. A program takes and returns all parts, laid end to end along the dimension named above; each array names one. Nothing has to cross between parts.
Inputs may be any that keep to these rules, and one draw needn't show every extreme that they name: `block_list`: entry -1 marks a screened-out slot; otherwise v = C * 8 + D. Pair v is owned by the device whose index along pairs is v modulo the number of devices along pairs. Among the slots of one device at most 2 non-empty ones name pairs of one owner, and some device sends 2 to every owner; every owner receives exactly 12 non-empty blocks.
All inputs are finite; a program needn't handle non-finite values.
Results may differ from the reference program's by a relative error of at most 0.0003.
Values sent between devices are 32-bit elements; how exact they have to be, the bound alone decides.
No kernel may reach another device: no remote copies, remote signals or barrier semaphores. Data moves between devices by JAX's collectives and lax.ppermute only.
A program may use at most 128 MiB of HBM per device.

```python
import jax
import jax.numpy as jnp
from jax import lax

BLK = 96
NB = 8
NAUX = 32
CAP = 2
NVP = 64
SLOTS = 32
KEEP = 8
LOAD = 12
PAIRS = 64
N_PAIRS = 16


def draw_block_list(key, part):
    key = jax.random.fold_in(key, 7)
    owners = N_PAIRS
    key_order, key_shift, key_weight, key_heavy, key_noise, key_pick = jax.random.split(key, 6)
    source = jnp.arange(owners, dtype=jnp.int32)[:, None]
    column = jnp.arange(SLOTS, dtype=jnp.int32)[None, :]
    shuffle = jax.random.randint(key_order, (owners, SLOTS), 0, 4096) * SLOTS + column
    order = jnp.argsort(jnp.argsort(shuffle, axis=1), axis=1).astype(jnp.int32)
    shift = jax.random.randint(key_shift, (), 0, owners)
    target = (source + order // CAP + shift) % owners
    within = order % CAP
    weight = jax.random.randint(key_weight, (owners,), 0, 4)
    heavy = jax.random.randint(key_heavy, (), 0, owners)
    weight = jnp.where(jnp.arange(owners) == heavy, 4, weight)
    noise = jax.random.randint(key_noise, (owners, SLOTS), 0, 64)
    score = (weight[:, None] * 64 + noise) * (owners * SLOTS) + source * SLOTS + column
    place = target * (owners * CAP) + source * CAP + within
    incoming = jnp.zeros((owners * owners * CAP,), jnp.int32).at[place.reshape(-1)].set(score.reshape(-1))
    incoming = incoming.reshape(owners, owners * CAP)
    above = jnp.sum((incoming[:, None, :] > incoming[:, :, None]).astype(jnp.int32), axis=2)
    chosen = (above < LOAD).reshape(-1)[place]
    pick = jax.random.randint(key_pick, (owners, SLOTS), 0, NVP // owners)
    virtual = target + owners * pick
    return jnp.where(chosen, virtual, -1).reshape(PAIRS, KEEP).astype(jnp.int32)


def steps_of(stream_key, extent, shards, smallest, largest):
    level, own = 1.0, jax.random.fold_in(stream_key, 6)
    for dim, shards_of in shards:
        steps = jnp.exp(jax.random.uniform(jax.random.fold_in(own, dim), (shards_of,), jnp.float32, smallest / len(shards), largest / len(shards)))
        level = level * jnp.repeat(steps, extent[dim] // shards_of).reshape([-1 if axis == dim else 1 for axis in range(len(extent))])
    return level


def centred(stream_key, extent, scale, limit, cuts=(), kind=jnp.bfloat16):
    factor_of = steps_of(stream_key, extent, cuts, -0.22, 0.18) if cuts else 1.0
    result = jax.random.normal(stream_key, extent, jnp.float32) * scale * factor_of
    return jnp.minimum(jnp.maximum(result, -limit), limit).astype(kind)


def setup_inputs(seed: int = 0, part: int = 0) -> dict:
    arg_keys = jax.random.split(jax.random.key(seed), 4)
    own_keys = jax.random.split(jax.random.fold_in(arg_keys[3], part), 4)
    return {
        "amplitudes": centred(own_keys[0], (PAIRS, KEEP, BLK * BLK), 1.0, 6.0, ((0, 16),), jnp.float32),
        "block_list": draw_block_list(jax.random.fold_in(jax.random.fold_in(arg_keys[3], part), 71), part),
        "factors": centred(own_keys[2], (NB * NAUX, BLK * BLK), 0.043, 0.26, ((0, 16),), jnp.float32),
    }


def ladder_batch(amps, left, right):
    half = jnp.einsum('ncd,npbd->npcb', amps, right, precision=lax.Precision.HIGHEST)
    return jnp.einsum('npac,npcb->nab', left, half, precision=lax.Precision.HIGHEST)


def reference(amplitudes, block_list, factors):
    cells = BLK * BLK
    flat = amplitudes.reshape(PAIRS * KEEP, cells)
    labels = block_list.reshape(PAIRS * KEEP)
    total = LOAD * N_PAIRS
    present = jnp.nonzero(labels >= 0, size=total, fill_value=0)[0].astype(jnp.int32)
    table = factors.reshape(NB, NAUX, BLK, BLK)

    def one_batch(rows):
        chosen = labels[rows]
        left = table[chosen // NB]
        right = table[chosen % NB]
        amps = flat[rows].reshape(-1, BLK, BLK)
        return ladder_batch(amps, left, right).reshape(-1, cells)

    results = lax.map(one_batch, present.reshape(-1, 16)).reshape(total, cells)
    output = jnp.zeros((PAIRS * KEEP, cells), jnp.float32).at[present].set(results)
    return output.reshape(PAIRS, KEEP, cells)
```

```python
import functools
import math

import jax
import jax.numpy as jnp
import numpy as np
from jax import lax
from jax.experimental import pallas as pl
from jax.experimental.pallas import tpu as pltpu
from jax.sharding import PartitionSpec as P

NB = 8
NAUX = 32
LANE = 128
UNROLL = 4
SPLIT = 2
GROUP = 64
BF = jnp.bfloat16
F32 = jnp.float32
NT = (((1,), (1,)), ((), ()))
VMEM_BYTES = 30 << 20
MICROS = (8, 10, 12, 8)


def split(x):
    hi = x.astype(BF)
    return hi, (x - hi.astype(F32)).astype(BF)


def unflatten(read, write, count, width):
    lane = lax.broadcasted_iota(jnp.int32, (count, LANE), 1)
    for m in range(width // 4):
        x0, x1, x2 = read(3 * m), read(3 * m + 1), read(3 * m + 2)
        write(4 * m, x0)
        write(4 * m + 1, pltpu.roll(jnp.where(lane >= 96, x0, x1), 32, 1))
        write(4 * m + 2, pltpu.roll(jnp.where(lane >= 64, x1, x2), 64, 1))
        write(4 * m + 3, pltpu.roll(x2, 96, 1))


def flatten(read, write, count, width):
    lane = lax.broadcasted_iota(jnp.int32, (count, LANE), 1)
    for m in range(width // 4):
        v0, v1, v2, v3 = (read(4 * m + r) for r in range(4))
        v1, v2, v3 = pltpu.roll(v1, 96, 1), pltpu.roll(v2, 64, 1), pltpu.roll(v3, 32, 1)
        write(3 * m, jnp.where(lane < 96, v0, v1))
        write(3 * m + 1, jnp.where(lane < 64, v1, v2))
        write(3 * m + 2, jnp.where(lane < 32, v2, v3))


def load_matrices(flat, mats, first, width):
    rows = flat.shape[0]
    step = min(8, rows)

    def group(g, carry):
        at = pl.multiple_of(g * step, step)
        base = pl.multiple_of((first + g * step) * width, 8)

        def read(j):
            return flat[pl.ds(at, step), j * LANE : (j + 1) * LANE]

        def write(e, v):
            mats[pl.ds(base + e, step, stride=width), :] = v

        unflatten(read, write, step, width)
        return carry

    lax.fori_loop(0, rows // step, group, 0)


def store_flat(mats, first, out, width, extra=None):
    rows = out.shape[0]
    step = min(8, rows)

    def group(g, carry):
        at = pl.multiple_of(g * step, step)
        base = pl.multiple_of((first + g * step) * width, 8)

        def read(e):
            return mats[pl.ds(base + e, step, stride=width), :]

        def write(j, v):
            where = (pl.ds(at, step), slice(j * LANE, (j + 1) * LANE))
            out[where] = v if extra is None else v + extra[where]

        flatten(read, write, step, width)
        return carry

    lax.fori_loop(0, rows // step, group, 0)


def fill_table(pieces, meta, tab, mats, width, per_block):
    for flat, offset, first, held in pieces:
        rows = flat.shape[0]
        load_matrices(flat, mats, 0, width)
        chip = meta[0, offset]
        block = chip // per_block
        lead = (chip % per_block) * held + first
        for i in range(rows):
            hi, lo = split(mats[i * width : (i + 1) * width, :])
            at = pl.ds(pl.multiple_of((lead + i) * LANE, LANE), LANE)
            tab[block, 0:width, at] = hi
            tab[block, width : 2 * width, at] = lo


def order_slots(labels, meta, chips, steps, order):
    for r in range(steps + 2):
        order[3, r] = 0

    def ready_of(v):
        c, d = jnp.maximum(v, 0) // NB, jnp.maximum(v, 0) % NB
        ready = jnp.maximum(jnp.maximum(meta[0, chips + c], meta[0, chips + d]), 1)
        return jnp.where(v >= 0, ready, steps + 1), c, d

    def tally(ref):
        def one(i, carry):
            ready, _, _ = ready_of(ref[i])
            order[3, ready] = order[3, ready] + 1
            return carry

        lax.fori_loop(0, ref.shape[0], one, 0)

    tally(labels[0][0])
    early = order[3, steps]
    for ref, _ in labels[1:]:
        tally(ref)
    total = 0
    for r in range(1, steps + 1):
        count = order[3, r]
        order[3, r] = total
        total = total + count
    order[3, steps + 1] = total
    early = early + order[3, steps]

    def put(ref, first):
        def one(i, carry):
            ready, c, d = ready_of(ref[i])
            n = order[3, ready]
            order[0, n] = first + i
            order[1, n] = c
            order[2, n] = d
            order[3, ready] = n + 1
            return carry

        lax.fori_loop(0, ref.shape[0], one, 0)

    for ref, first in labels:
        put(ref, first)
    for r in range(1, steps):
        order[3, r] = order[3, r] // UNROLL
    order[3, 0] = 0
    order[3, steps] = (total + UNROLL - 1) // UNROLL
    order[3, steps + 1] = (early + UNROLL - 1) // UNROLL
    return total


def pad_order(order, total, dummy):
    for u in range(UNROLL - 1):
        order[0, total + u] = dummy
        order[1, total + u] = 0
        order[2, total + u] = 0


def run_slots(low, high, order, tab, amp, acc, wide, half, width):
    cols = tab.shape[2] // LANE
    per = cols // SPLIT
    for u in range(UNROLL):
        for at in range(0, 2 * LANE, LANE):
            wide[u, at + width : at + LANE, :] = jnp.zeros((LANE - width, wide.shape[2]), BF)
            wide[u, at : at + width, :] = jnp.zeros((width, wide.shape[2]), BF)
            half[u, at + width : at + LANE, :] = jnp.zeros((LANE - width, half.shape[2]), BF)

    def some(i, carry):
        ids = [tuple(order[k, i * UNROLL + u] for k in range(3)) for u in range(UNROLL)]
        for u, (s, _, _) in enumerate(ids):
            t = amp[pl.ds(pl.multiple_of(s * width, 8), width), :]
            hi, lo = split(t)
            hi, lo = hi[:, :width], lo[:, :width]
            wide[u, 0:width, 0:width] = hi
            wide[u, 0:width, LANE : LANE + width] = hi
            wide[u, LANE : LANE + width, 0:width] = lo
            wide[u, LANE : LANE + width, LANE : LANE + width] = lo
        for g in range(SPLIT):
            for u, (_, _, d) in enumerate(ids):
                left = []
                for p in range(g * per, (g + 1) * per):
                    at = slice(p * LANE, (p + 1) * LANE)
                    left.append(jnp.concatenate([tab[d, 0:width, at], tab[d, width : 2 * width, at]], axis=1))
                r = lax.dot_general(jnp.concatenate(left, axis=0), wide[u], NT, preferred_element_type=F32)
                hi, lo = split(r[:, :LANE] + r[:, LANE:])
                for j, p in enumerate(range(g * per, (g + 1) * per)):
                    at = slice(p * LANE, (p + 1) * LANE)
                    half[u, 0:width, at] = hi[j * width : (j + 1) * width]
                    half[u, LANE : LANE + width, at] = lo[j * width : (j + 1) * width]
        for u, (s, c, _) in enumerate(ids):
            o = lax.dot_general(tab[c], half[u], NT, preferred_element_type=F32)
            o = (o[:width, :LANE] + o[width:, :LANE]) + o[:width, LANE:]
            acc[pl.ds(pl.multiple_of(s * width, 8), width), :] = o
        return carry

    lax.fori_loop(low, high, some, 0)


def scratch(cols, width, rows):
    return [
        pltpu.VMEM((max(rows, 1) * width, LANE), F32),
        pltpu.VMEM((UNROLL, 2 * LANE, 2 * LANE), BF),
        pltpu.VMEM((UNROLL, 2 * LANE, cols * LANE), BF),
    ]


def resident(x):
    return pltpu.with_memory_space_constraint(x, pltpu.VMEM)


def call(body, ins, keep, outs, width, rows, name, micros):
    vm, sm = pl.BlockSpec(memory_space=pltpu.VMEM), pl.BlockSpec(memory_space=pltpu.SMEM)
    arrays = [x for x, _ in ins]
    specs = [sm if scalars else vm for _, scalars in ins]
    shapes, aliases, olds = [], {}, 0
    for i, x in enumerate(keep):
        if isinstance(x, jax.Array):
            aliases[len(arrays)] = i
            arrays.append(resident(x))
            specs.append(vm)
            olds += 1
            shapes.append(pltpu.VMEM(x.shape, x.dtype))
        else:
            shapes.append(x)
    specs_out = [vm] * len(keep) + [sm if x.dtype == jnp.int32 else vm for x in outs]

    def kernel(*refs):
        refs = list(refs)
        given, refs = refs[: len(ins)], refs[len(ins) + olds :]
        states, refs = refs[: len(keep)], refs[len(keep) :]
        made, refs = refs[: len(outs)], refs[len(outs) :]
        body(given, states, made, *refs)

    results = pl.pallas_call(
        kernel,
        out_shape=shapes + list(outs),
        in_specs=specs,
        out_specs=specs_out,
        input_output_aliases=aliases,
        scratch_shapes=scratch(NAUX // 2, width, rows),
        compiler_params=pltpu.CompilerParams(vmem_limit_bytes=VMEM_BYTES),
        cost_estimate=pl.CostEstimate(flops=int(micros * 1e9), bytes_accessed=int(micros * 3e6), transcendentals=0),
        name=name,
    )(*arrays)
    return results[: len(keep)], results[len(keep) :]


def final_kernel(first, width, acc, got, out):
    store_flat(acc, first, out, width, got)


def final_call(acc, got, first, width):
    vm = pl.BlockSpec(memory_space=pltpu.VMEM)
    return pl.pallas_call(
        functools.partial(final_kernel, first, width),
        out_shape=jax.ShapeDtypeStruct(got.shape, F32),
        in_specs=[vm, vm],
        out_specs=vm,
        compiler_params=pltpu.CompilerParams(vmem_limit_bytes=VMEM_BYTES),
        name="combine",
    )(resident(acc), got)


def ring_order(mesh):
    devices = mesh.devices.reshape(mesh.shape["groups"], mesh.shape["pairs"])[0, ::2]
    count = len(devices)
    places = [tuple(getattr(d, "coords", None) or (i, 0, 0)) for i, d in enumerate(devices)]
    spread = [sorted({p[a] for p in places}) for a in range(len(places[0]))]
    varying = [a for a in range(len(spread)) if len(spread[a]) > 1]
    if len(varying) == 2 and min(len(spread[a]) for a in varying) == 2:
        short, long = sorted(varying, key=lambda a: len(spread[a]))
        up = sorted((i for i in range(count) if places[i][short] == spread[short][0]), key=lambda i: places[i][long])
        down = sorted((i for i in range(count) if places[i][short] != spread[short][0]), key=lambda i: -places[i][long])
        return up + down
    return list(range(count))


def shards(ring, amplitudes, block_list, factors):
    pair_rows, keep, cells = amplitudes.shape
    width = math.isqrt(cells)
    slots = pair_rows * keep
    held = factors.shape[0]
    chips = len(ring)
    steps = chips // 2
    cut = held // 2
    per_block = NAUX // (2 * held)

    place = {c: i for i, c in enumerate(ring)}
    table = np.zeros((chips, chips + NB), np.int32)
    for c in range(chips):
        for j in range(chips):
            table[c, j] = ring[(place[c] + j) % chips]
        for j in range(chips):
            far = min(j, chips - j)
            b = table[c, j] // per_block
            table[c, chips + b] = max(table[c, chips + b], far)

    def shift(x, by):
        pairs = [
            (2 * ring[i] + core, 2 * ring[(i + by) % chips] + core) for i in range(chips) for core in range(2)
        ]
        return lax.ppermute(x, "pairs", pairs)

    def swap(x):
        return lax.ppermute(x, "pairs", [(i, i ^ 1) for i in range(2 * chips)])

    flat = amplitudes.reshape(slots, cells)
    labels = block_list.reshape(slots)
    row = lax.axis_index("pairs") // 2
    meta = lax.dynamic_slice(jnp.asarray(table), (row, 0), (1, chips + NB))

    up = [factors[:cut], factors[cut:]]
    down = list(up)
    arrivals = [[(up[0], 0, 0), (up[1], 0, cut)]]
    for k in range(1, steps + 1):
        if k < steps:
            up = [shift(x, 1) for x in up]
            down = [shift(x, -1) for x in down]
            arrivals.append(
                [(x, chips - k, h * cut) for h, x in enumerate(up)] + [(x, k, h * cut) for h, x in enumerate(down)]
            )
        else:
            arrivals.append([(shift(up[0], 1), steps, 0), (shift(down[1], -1), steps, cut)])
    other_flat, other_labels = swap(flat), swap(labels)

    cols = NAUX // 2
    table_shape = pltpu.VMEM((NB, 2 * width, cols * LANE), BF)

    def fill(refs, pieces, meta_ref, tab, mats):
        fill_table([(ref, o, f, held) for ref, (_, o, f) in zip(refs, pieces)], meta_ref, tab, mats, width, per_block)

    def piece_ins(pieces):
        return [(x, False) for x, _, _ in pieces]

    if 2 * slots <= GROUP:
        matrices = pltpu.VMEM(((2 * slots + 1) * width, LANE), F32)
        order_shape = jax.ShapeDtypeStruct((4, 2 * slots + max(UNROLL, steps + 2)), jnp.int32)
        state, order = [table_shape, matrices, matrices], None
        for k in range(1, steps + 1):
            pieces = (arrivals[0] if k == 1 else []) + arrivals[k]
            opening = [(labels, True), (other_labels, True), (flat, False), (other_flat, False)] if k == 1 else [(order, True)]
            closing = [jax.ShapeDtypeStruct(flat.shape, F32)] if k == steps else []

            def body(given, states, made, mats, wide, half, k=k, pieces=pieces, n=len(opening)):
                meta_ref, extra, refs = given[0], given[1 : 1 + n], given[1 + n :]
                tab, amp, acc = states
                fill(refs, pieces, meta_ref, tab, mats)
                if k == 1:
                    own_l, other_l, own, other = extra
                    listed = made[0]
                    total = order_slots([(other_l, slots), (own_l, 0)], meta_ref, chips, steps, listed)
                    pad_order(listed, total, 2 * slots)
                    acc[...] = jnp.zeros_like(acc)
                    load_matrices(own, amp, 0, width)
                    load_matrices(other, amp, slots, width)
                else:
                    listed = extra[0]
                high = listed[3, k] if k < steps else listed[3, steps + 1]
                run_slots(listed[3, k - 1], high, listed, tab, amp, acc, wide, half, width)
                if k == steps:
                    store_flat(acc, slots, made[-1], width)

            state, made = call(
                body,
                [(meta, True)] + opening + piece_ins(pieces),
                state,
                ([order_shape] if k == 1 else []) + closing,
                width,
                cut,
                f"slots_step_{k}",
                MICROS[min(k, len(MICROS)) - 1],
            )
            if k == 1:
                order = made[0]
        back = swap(made[-1])

        def last(given, states, made, mats, wide, half):
            run_slots(given[0][3, steps + 1], given[0][3, steps], given[0], *states, wide, half, width)

        state, _ = call(last, [(order, True)], state, [], width, 1, "slots_own", MICROS[-1])
        result = final_call(state[2], back, 0, width)
    else:
        state = [table_shape]
        for k in range(1, steps + 1):
            pieces = (arrivals[0] if k == 1 else []) + arrivals[k]

            def body(given, states, made, mats, wide, half, pieces=pieces):
                fill(given[1:], pieces, given[0], states[0], mats)

            state, _ = call(body, [(meta, True)] + piece_ins(pieces), state, [], width, cut, f"table_step_{k}", 2)

        def group(given, states, made, mats, wide, half):
            meta_ref, names, rows = given
            result_ref, listed = made[:2]
            count = rows.shape[0]
            amp, acc = states[1:]
            total = order_slots([(names, 0)], meta_ref, chips, steps, listed)
            pad_order(listed, total, count)
            acc[...] = jnp.zeros_like(acc)
            load_matrices(rows, amp, 0, width)
            run_slots(0, listed[3, steps], listed, states[0], amp, acc, wide, half, width)
            store_flat(acc, 0, result_ref, width)

        def grouped(rows, names):
            nonlocal state
            results = []
            for g in range(0, slots, GROUP):
                count = min(GROUP, slots - g)
                matrices = pltpu.VMEM(((count + 1) * width, LANE), F32)
                kept, made = call(
                    group,
                    [(meta, True), (names[g : g + count], True), (rows[g : g + count], False)],
                    [state[0], matrices, matrices],
                    [
                        jax.ShapeDtypeStruct((count, cells), F32),
                        jax.ShapeDtypeStruct((4, count + max(UNROLL, steps + 2)), jnp.int32),
                    ],
                    width,
                    1,
                    f"slots_group_{g}",
                    20,
                )
                state = kept[:1]
                results.append(made[0])
            return jnp.concatenate(results) if len(results) > 1 else results[0]

        back = swap(grouped(other_flat, other_labels))
        result = grouped(flat, labels) + back
    return result.reshape(pair_rows, keep, cells)


def solution(mesh):
    return jax.shard_map(
        functools.partial(shards, ring_order(mesh)),
        mesh=mesh,
        in_specs=(
            P(("groups", "pairs"), None, None),
            P(("groups", "pairs"), None),
            P(("groups", "pairs"), None),
        ),
        out_specs=P(("groups", "pairs"), None, None),
        check_vma=False,
    )
```

```python
import functools
import math

import jax
import jax.numpy as jnp
import numpy as np
from jax import lax
from jax.experimental import pallas as pl
from jax.experimental.pallas import tpu as pltpu
from jax.sharding import PartitionSpec as P

NB = 8
NAUX = 32
LANE = 128
UNROLL = 4
SPLIT = 2
GROUP = 64
BF = jnp.bfloat16
F32 = jnp.float32
NT = (((1,), (1,)), ((), ()))
VMEM_BYTES = 20 << 20
MICROS = (4, 8, 10, 12, 8)
TOKEN = jax.ShapeDtypeStruct((8, LANE), F32)


def split(x):
    hi = x.astype(BF)
    return hi, (x - hi.astype(F32)).astype(BF)


def unflatten(read, write, count, width):
    lane = lax.broadcasted_iota(jnp.int32, (count, LANE), 1)
    for m in range(width // 4):
        x0, x1, x2 = read(3 * m), read(3 * m + 1), read(3 * m + 2)
        write(4 * m, x0)
        write(4 * m + 1, pltpu.roll(jnp.where(lane >= 96, x0, x1), 32, 1))
        write(4 * m + 2, pltpu.roll(jnp.where(lane >= 64, x1, x2), 64, 1))
        write(4 * m + 3, pltpu.roll(x2, 96, 1))


def pack(v0, v1, v2, v3):
    lane = lax.broadcasted_iota(jnp.int32, v0.shape, 1)
    v1, v2, v3 = pltpu.roll(v1, 96, 1), pltpu.roll(v2, 64, 1), pltpu.roll(v3, 32, 1)
    return jnp.where(lane < 96, v0, v1), jnp.where(lane < 64, v1, v2), jnp.where(lane < 32, v2, v3)


def flatten(read, write, width):
    for m in range(width // 4):
        for j, y in enumerate(pack(*(read(4 * m + r) for r in range(4)))):
            write(3 * m + j, y)


def load_matrices(flat, mats, first, width):
    rows = flat.shape[0]
    step = min(8, rows)

    def group(g, carry):
        at = pl.multiple_of(g * step, step)
        base = pl.multiple_of((first + g * step) * width, 8)

        def read(j):
            return flat[pl.ds(at, step), j * LANE : (j + 1) * LANE]

        def write(e, v):
            mats[pl.ds(base + e, step, stride=width), :] = v

        unflatten(read, write, step, width)
        return carry

    lax.fori_loop(0, rows // step, group, 0)


def store_flat(mats, first, out, width, extra=None):
    rows = out.shape[0]
    step = min(8, rows)

    def group(g, carry):
        at = pl.multiple_of(g * step, step)
        base = pl.multiple_of((first + g * step) * width, 8)

        def read(e):
            return mats[pl.ds(base + e, step, stride=width), :]

        def write(j, v):
            where = (pl.ds(at, step), slice(j * LANE, (j + 1) * LANE))
            out[where] = v if extra is None else v + extra[where]

        flatten(read, write, width)
        return carry

    lax.fori_loop(0, rows // step, group, 0)


def fill_table(pieces, meta, tabs, mats, width, per_block):
    right, left = tabs
    for flat, offset, first, held in pieces:
        rows = flat.shape[0]
        load_matrices(flat, mats, 0, width)
        chip = meta[0, offset]
        block = chip // per_block
        lead = (chip % per_block) * held + first
        for i in range(0, rows, 4):
            four = [mats[(i + r) * width : (i + r + 1) * width, :] for r in range(4)]
            for r, x in enumerate(four):
                hi, lo = split(x)
                at = pl.multiple_of((lead + i + r) * LANE, LANE)
                right[block, 0:width, pl.ds(at, LANE)] = hi
                right[block, width : 2 * width, pl.ds(at, LANE)] = lo
            for j, y in enumerate(pack(*four)):
                hi, lo = split(y)
                at = pl.multiple_of(((lead + i) // 4 * 3 + j) * LANE, LANE)
                left[block, 0:width, pl.ds(at, LANE)] = hi
                left[block, width : 2 * width, pl.ds(at, LANE)] = lo


def order_slots(labels, meta, chips, steps, order):
    for r in range(steps + 2):
        order[3, r] = 0

    def ready_of(v):
        c, d = jnp.maximum(v, 0) // NB, jnp.maximum(v, 0) % NB
        ready = jnp.maximum(jnp.maximum(meta[0, chips + c], meta[0, chips + d]), 1)
        return jnp.where(v >= 0, ready, steps + 1), c, d

    def tally(ref):
        def one(i, carry):
            ready, _, _ = ready_of(ref[i])
            order[3, ready] = order[3, ready] + 1
            return carry

        lax.fori_loop(0, ref.shape[0], one, 0)

    tally(labels[0][0])
    early = order[3, steps]
    for ref, _ in labels[1:]:
        tally(ref)
    total = 0
    for r in range(1, steps + 1):
        count = order[3, r]
        order[3, r] = total
        total = total + count
    order[3, steps + 1] = total
    early = early + order[3, steps]

    def put(ref, first):
        def one(i, carry):
            ready, c, d = ready_of(ref[i])
            n = order[3, ready]
            order[0, n] = first + i
            order[1, n] = c
            order[2, n] = d
            order[3, ready] = n + 1
            return carry

        lax.fori_loop(0, ref.shape[0], one, 0)

    for ref, first in labels:
        put(ref, first)
    for r in range(1, steps):
        order[3, r] = order[3, r] // UNROLL
    order[3, 0] = 0
    order[3, steps] = (total + UNROLL - 1) // UNROLL
    order[3, steps + 1] = (early + UNROLL - 1) // UNROLL
    return total


def pad_order(order, total, dummy):
    for u in range(UNROLL - 1):
        order[0, total + u] = dummy
        order[1, total + u] = 0
        order[2, total + u] = 0


def run_slots(low, high, order, right, left, amp, acc, wide, half, width):
    cols = right.shape[2] // LANE
    per = cols // SPLIT
    wide[...] = jnp.zeros_like(wide)

    def some(i, carry):
        ids = [tuple(order[k, i * UNROLL + u] for k in range(3)) for u in range(UNROLL)]
        for u, (s, _, _) in enumerate(ids):
            t = amp[pl.ds(pl.multiple_of(s * width, 8), width), :]
            hi, lo = split(t)
            hi, lo = hi[:, :width], lo[:, :width]
            wide[u, 0:width, 0:width] = hi
            wide[u, 0:width, LANE : LANE + width] = hi
            wide[u, LANE : LANE + width, 0:width] = lo
            wide[u, LANE : LANE + width, LANE : LANE + width] = lo
        for g in range(SPLIT):
            for u, (_, _, d) in enumerate(ids):
                rows = []
                for p in range(g * per, (g + 1) * per):
                    at = slice(p * LANE, (p + 1) * LANE)
                    rows.append(jnp.concatenate([right[d, 0:width, at], right[d, width : 2 * width, at]], axis=1))
                r = lax.dot_general(jnp.concatenate(rows, axis=0), wide[u], NT, preferred_element_type=F32)
                r = r[:, :LANE] + r[:, LANE:]
                for j in range(0, per, 4):
                    for k, y in enumerate(pack(*(r[(j + q) * width : (j + q + 1) * width] for q in range(4)))):
                        hi, lo = split(y)
                        at = ((g * per + j) // 4 * 3 + k) * LANE
                        half[u, 0:width, at : at + LANE] = hi
                        half[u, width : 2 * width, at : at + LANE] = lo
        for u, (s, c, _) in enumerate(ids):
            o = lax.dot_general(left[c], half[u], NT, preferred_element_type=F32)
            o = o[:width, :width] + o[width:, :width] + o[:width, width:]
            acc[pl.ds(pl.multiple_of(s * width, 8), width), 0:width] = o
        return carry

    lax.fori_loop(low, high, some, 0)


def scratch(cols, width, rows):
    return [
        pltpu.VMEM((max(rows, 1) * width, LANE), F32),
        pltpu.VMEM((UNROLL, 2 * LANE, 2 * LANE), BF),
        pltpu.VMEM((UNROLL, 2 * width, cols * width), BF),
    ]


def resident(x):
    return pltpu.with_memory_space_constraint(x, pltpu.VMEM)


def call(body, ins, keep, outs, width, rows, name, micros):
    vm, sm = pl.BlockSpec(memory_space=pltpu.VMEM), pl.BlockSpec(memory_space=pltpu.SMEM)
    arrays = [x for x, _ in ins]
    specs = [sm if scalars else vm for _, scalars in ins]
    shapes, aliases, olds = [], {}, 0
    for i, x in enumerate(keep):
        if isinstance(x, jax.Array):
            aliases[len(arrays)] = i
            arrays.append(resident(x))
            specs.append(vm)
            olds += 1
            shapes.append(pltpu.VMEM(x.shape, x.dtype))
        else:
            shapes.append(x)
    specs_out = [vm] * len(keep) + [sm if x.dtype == jnp.int32 else vm for x in outs]

    def kernel(*refs):
        refs = list(refs)
        given, refs = refs[: len(ins)], refs[len(ins) + olds :]
        states, refs = refs[: len(keep)], refs[len(keep) :]
        made, refs = refs[: len(outs)], refs[len(outs) :]
        body(given, states, made, *refs)

    results = pl.pallas_call(
        kernel,
        out_shape=shapes + list(outs),
        in_specs=specs,
        out_specs=specs_out,
        input_output_aliases=aliases,
        scratch_shapes=scratch(NAUX // 2, width, rows),
        compiler_params=pltpu.CompilerParams(vmem_limit_bytes=VMEM_BYTES),
        cost_estimate=pl.CostEstimate(flops=int(micros * 1e9), bytes_accessed=int(micros * 3e6), transcendentals=0),
        name=name,
    )(*arrays)
    return results[: len(keep)], results[len(keep) :]


def after(arrays, token):
    anywhere = pl.BlockSpec(memory_space=pl.ANY)
    return pl.pallas_call(
        lambda *refs: None,
        out_shape=[jax.ShapeDtypeStruct(x.shape, x.dtype) for x in arrays],
        in_specs=[anywhere] * (len(arrays) + 1),
        out_specs=[anywhere] * len(arrays),
        input_output_aliases={i: i for i in range(len(arrays))},
        compiler_params=pltpu.CompilerParams(vmem_limit_bytes=1 << 20),
        name="gate",
    )(*arrays, token)


def final_kernel(first, width, acc, got, out):
    store_flat(acc, first, out, width, got)


def final_call(acc, got, first, width):
    vm = pl.BlockSpec(memory_space=pltpu.VMEM)
    return pl.pallas_call(
        functools.partial(final_kernel, first, width),
        out_shape=jax.ShapeDtypeStruct(got.shape, F32),
        in_specs=[vm, vm],
        out_specs=vm,
        compiler_params=pltpu.CompilerParams(vmem_limit_bytes=VMEM_BYTES),
        name="combine",
    )(resident(acc), got)


def ring_order(mesh):
    devices = mesh.devices.reshape(mesh.shape["groups"], mesh.shape["pairs"])[0, ::2]
    count = len(devices)
    places = [tuple(getattr(d, "coords", None) or (i, 0, 0)) for i, d in enumerate(devices)]
    spread = [sorted({p[a] for p in places}) for a in range(len(places[0]))]
    varying = [a for a in range(len(spread)) if len(spread[a]) > 1]
    if len(varying) == 2 and min(len(spread[a]) for a in varying) == 2:
        short, long = sorted(varying, key=lambda a: len(spread[a]))
        up = sorted((i for i in range(count) if places[i][short] == spread[short][0]), key=lambda i: places[i][long])
        down = sorted((i for i in range(count) if places[i][short] != spread[short][0]), key=lambda i: -places[i][long])
        return up + down
    return list(range(count))


def shards(ring, amplitudes, block_list, factors):
    pair_rows, keep, cells = amplitudes.shape
    width = math.isqrt(cells)
    slots = pair_rows * keep
    held = factors.shape[0]
    chips = len(ring)
    steps = chips // 2
    parts = 2 if held % 8 == 0 else 1
    cut = held // parts
    per_block = NAUX // (2 * held)

    place = {c: i for i, c in enumerate(ring)}
    table = np.zeros((chips, chips + NB), np.int32)
    for c in range(chips):
        for j in range(chips):
            table[c, j] = ring[(place[c] + j) % chips]
        for j in range(chips):
            far = min(j, chips - j)
            b = table[c, j] // per_block
            table[c, chips + b] = max(table[c, chips + b], far)

    def shift(x, by):
        pairs = [
            (2 * ring[i] + core, 2 * ring[(i + by) % chips] + core) for i in range(chips) for core in range(2)
        ]
        return lax.ppermute(x, "pairs", pairs)

    def swap(x):
        return lax.ppermute(x, "pairs", [(i, i ^ 1) for i in range(2 * chips)])

    flat = amplitudes.reshape(slots, cells)
    labels = block_list.reshape(slots)
    row = lax.axis_index("pairs") // 2
    meta = lax.dynamic_slice(jnp.asarray(table), (row, 0), (1, chips + NB))

    up = [factors[i * cut : (i + 1) * cut] for i in range(parts)]
    down = list(up)
    arrivals = [[(x, 0, h * cut) for h, x in enumerate(up)]]
    cols = NAUX // 2
    tables = [pltpu.VMEM((NB, 2 * width, cols * LANE), BF), pltpu.VMEM((NB, 2 * width, cols * width), BF)]

    def fill(refs, pieces, meta_ref, tabs, mats):
        fill_table([(ref, o, f, held) for ref, (_, o, f) in zip(refs, pieces)], meta_ref, tabs, mats, width, per_block)

    def piece_ins(pieces):
        return [(x, False) for x, _, _ in pieces]

    def travel(k):
        nonlocal up, down
        if k < steps:
            up = [shift(x, 1) for x in up]
            down = [shift(x, -1) for x in down]
            arrivals.append(
                [(x, chips - k, h * cut) for h, x in enumerate(up)] + [(x, k, h * cut) for h, x in enumerate(down)]
            )
        else:
            last = [(shift(up[0], 1), steps, 0)]
            arrivals.append(last + ([(shift(down[1], -1), steps, cut)] if parts == 2 else []))

    if 2 * slots <= GROUP:
        matrices = pltpu.VMEM(((2 * slots + 1) * width, LANE), F32)
        order_shape = jax.ShapeDtypeStruct((4, 2 * slots + max(UNROLL, steps + 2)), jnp.int32)
        other_flat, other_labels = swap(flat), swap(labels)
        travel(1)

        def prepare(given, states, made, mats, wide, half):
            meta_ref, own_l, other_l, own, other = given[:5]
            total = order_slots([(other_l, slots), (own_l, 0)], meta_ref, chips, steps, made[0])
            pad_order(made[0], total, 2 * slots)
            states[3][...] = jnp.zeros_like(states[3])
            made[1][...] = jnp.zeros_like(made[1])
            load_matrices(own, states[2], 0, width)
            load_matrices(other, states[2], slots, width)
            fill(given[5:], arrivals[0], meta_ref, states[:2], mats)

        state, (order, token) = call(
            prepare,
            [(meta, True), (labels, True), (other_labels, True), (flat, False), (other_flat, False)]
            + piece_ins(arrivals[0]),
            tables + [matrices, matrices],
            [order_shape, TOKEN],
            width,
            cut,
            "prepare",
            MICROS[0],
        )
        for k in range(1, steps + 1):
            if k < steps:
                for i in range(parts):
                    up[i], down[i] = after([up[i], down[i]], token)
                arrivals[k] = [
                    (x, chips - k, h * cut) for h, x in enumerate(up)
                ] + [(x, k, h * cut) for h, x in enumerate(down)]
                travel(k + 1)
            closing = [jax.ShapeDtypeStruct(flat.shape, F32)] if k == steps else [TOKEN]

            def body(given, states, made, mats, wide, half, k=k):
                meta_ref, listed = given[:2]
                fill(given[2:], arrivals[k], meta_ref, states[:2], mats)
                high = listed[3, k] if k < steps else listed[3, steps + 1]
                run_slots(listed[3, k - 1], high, listed, *states, wide, half, width)
                if k == steps:
                    store_flat(states[3], slots, made[0], width)
                else:
                    made[0][...] = jnp.zeros_like(made[0])

            state, (token,) = call(
                body,
                [(meta, True), (order, True)] + piece_ins(arrivals[k]),
                state,
                closing,
                width,
                cut,
                f"slots_step_{k}",
                MICROS[min(k, len(MICROS) - 1)],
            )
        back = swap(token)

        def last(given, states, made, mats, wide, half):
            run_slots(given[0][3, steps + 1], given[0][3, steps], given[0], *states, wide, half, width)

        state, _ = call(last, [(order, True)], state, [], width, 1, "slots_own", MICROS[-1])
        result = final_call(state[3], back, 0, width)
    else:
        state = tables
        for k in range(1, steps + 1):
            travel(k)
            pieces = (arrivals[0] if k == 1 else []) + arrivals[k]

            def body(given, states, made, mats, wide, half, pieces=pieces):
                fill(given[1:], pieces, given[0], states, mats)

            state, _ = call(body, [(meta, True)] + piece_ins(pieces), state, [], width, cut, f"table_step_{k}", 2)

        def group(given, states, made, mats, wide, half):
            meta_ref, names, rows = given
            result_ref, listed = made[:2]
            count = rows.shape[0]
            amp, acc = states[2:]
            total = order_slots([(names, 0)], meta_ref, chips, steps, listed)
            pad_order(listed, total, count)
            acc[...] = jnp.zeros_like(acc)
            load_matrices(rows, amp, 0, width)
            run_slots(0, listed[3, steps], listed, *states, wide, half, width)
            store_flat(acc, 0, result_ref, width)

        def grouped(rows, names):
            nonlocal state
            results = []
            for g in range(0, slots, GROUP):
                count = min(GROUP, slots - g)
                matrices = pltpu.VMEM(((count + 1) * width, LANE), F32)
                kept, made = call(
                    group,
                    [(meta, True), (names[g : g + count], True), (rows[g : g + count], False)],
                    [*state, matrices, matrices],
                    [
                        jax.ShapeDtypeStruct((count, cells), F32),
                        jax.ShapeDtypeStruct((4, count + max(UNROLL, steps + 2)), jnp.int32),
                    ],
                    width,
                    1,
                    f"slots_group_{g}",
                    20,
                )
                state = kept[:2]
                results.append(made[0])
            return jnp.concatenate(results) if len(results) > 1 else results[0]

        back = swap(grouped(swap(flat), swap(labels)))
        result = grouped(flat, labels) + back
    return result.reshape(pair_rows, keep, cells)


def solution(mesh):
    return jax.shard_map(
        functools.partial(shards, ring_order(mesh)),
        mesh=mesh,
        in_specs=(
            P(("groups", "pairs"), None, None),
            P(("groups", "pairs"), None),
            P(("groups", "pairs"), None),
        ),
        out_specs=P(("groups", "pairs"), None, None),
        check_vma=False,
    )
```

```python
import functools
import math

import jax
import jax.numpy as jnp
import numpy as np
from jax import lax
from jax.experimental import pallas as pl
from jax.experimental.pallas import tpu as pltpu
from jax.sharding import PartitionSpec as P

NB = 8
NAUX = 32
LANE = 128
UNROLL = 4
PER = 8
GROUP = 64
BF = jnp.bfloat16
F32 = jnp.float32
NN = (((1,), (0,)), ((), ()))
VMEM_BYTES = 16 << 20
TOKEN = jax.ShapeDtypeStruct((8, LANE), F32)


def split(x):
    hi = x.astype(BF)
    return hi, (x - hi.astype(F32)).astype(BF)


def unpack(y0, y1, y2):
    lane = lax.broadcasted_iota(jnp.int32, y0.shape, 1)
    v1, v2 = jnp.where(lane >= 96, y0, y1), jnp.where(lane >= 64, y1, y2)
    return y0, pltpu.roll(v1, 32, 1), pltpu.roll(v2, 64, 1), pltpu.roll(y2, 96, 1)


def unflatten(read, write, width):
    for m in range(width // 4):
        for r, v in enumerate(unpack(*(read(3 * m + j) for j in range(3)))):
            write(4 * m + r, v)


def pack(v0, v1, v2, v3):
    lane = lax.broadcasted_iota(jnp.int32, v0.shape, 1)
    v1, v2, v3 = pltpu.roll(v1, 96, 1), pltpu.roll(v2, 64, 1), pltpu.roll(v3, 32, 1)
    return jnp.where(lane < 96, v0, v1), jnp.where(lane < 64, v1, v2), jnp.where(lane < 32, v2, v3)


def flatten(read, write, width):
    for m in range(width // 4):
        for j, y in enumerate(pack(*(read(4 * m + r) for r in range(4)))):
            write(3 * m + j, y)


def load_matrices(flat, mats, first, width):
    rows = flat.shape[0]
    step = min(8, rows)

    def group(g, carry):
        at = pl.multiple_of(g * step, step)
        base = pl.multiple_of((first + g * step) * width, 8)

        def read(j):
            return flat[pl.ds(at, step), j * LANE : (j + 1) * LANE]

        def write(e, v):
            mats[pl.ds(base + e, step, stride=width), :] = v

        unflatten(read, write, width)
        return carry

    lax.fori_loop(0, rows // step, group, 0)


def store_flat(mats, first, out, width):
    rows = out.shape[0]
    step = min(8, rows)

    def group(g, carry):
        at = pl.multiple_of(g * step, step)
        base = pl.multiple_of((first + g * step) * width, 8)

        def read(e):
            return mats[pl.ds(base + e, step, stride=width), :]

        def write(j, v):
            out[pl.ds(at, step), j * LANE : (j + 1) * LANE] = v

        flatten(read, write, width)
        return carry

    lax.fori_loop(0, rows // step, group, 0)


def fill_table(pieces, meta, tabs, mats, width, per_block):
    right, left = tabs
    for flat, offset, first, held in pieces:
        rows = flat.shape[0]
        load_matrices(flat, mats, 0, width)
        chip = meta[0, offset]
        block = chip // per_block
        lead = (chip % per_block) * held + first
        for i in range(0, rows, 4):
            four = [mats[(i + r) * width : (i + r + 1) * width, :] for r in range(4)]
            blank = jnp.zeros((width, LANE - width), F32)
            turned = [jnp.concatenate([x.T[:width], blank], axis=1) for x in four]
            for table, matrices in ((left, four), (right, turned)):
                for j, y in enumerate(pack(*matrices)):
                    hi, lo = split(y)
                    at = pl.multiple_of(((lead + i) // 4 * 3 + j) * LANE, LANE)
                    table[block, 0:width, pl.ds(at, LANE)] = hi
                    table[block, width : 2 * width, pl.ds(at, LANE)] = lo


def order_slots(labels, meta, chips, steps, order):
    for r in range(steps + 2):
        order[3, r] = 0

    def ready_of(v):
        c, d = jnp.maximum(v, 0) >> 3, jnp.maximum(v, 0) & 7
        ready = jnp.maximum(jnp.maximum(meta[0, chips + c], meta[0, chips + d]), 1)
        return jnp.where(v >= 0, ready, steps + 1), c, d

    def tally(ref):
        def one(i, carry):
            ready, _, _ = ready_of(ref[i])
            order[3, ready] = order[3, ready] + 1
            return carry

        lax.fori_loop(0, ref.shape[0], one, 0, unroll=8)

    tally(labels[0][0])
    early = order[3, steps]
    for ref, _ in labels[1:]:
        tally(ref)
    total = 0
    for r in range(1, steps + 1):
        count = order[3, r]
        order[3, r] = total
        total = total + count
    order[3, steps + 1] = total
    early = early + order[3, steps]

    def put(ref, first):
        def one(i, carry):
            ready, c, d = ready_of(ref[i])
            n = order[3, ready]
            order[0, n] = first + i
            order[1, n] = c
            order[2, n] = d
            order[3, ready] = n + 1
            return carry

        lax.fori_loop(0, ref.shape[0], one, 0, unroll=8)

    for ref, first in labels:
        put(ref, first)
    for r in range(1, steps):
        order[3, r] = order[3, r] // UNROLL
    order[3, 0] = 0
    order[3, steps] = (total + UNROLL - 1) // UNROLL
    order[3, steps + 1] = (early + UNROLL - 1) // UNROLL
    return total


def pad_order(order, total, dummy):
    for u in range(UNROLL - 1):
        order[0, total + u] = dummy
        order[1, total + u] = 0
        order[2, total + u] = 0


def run_slots(low, high, order, right, left, amp, acc, wide, half, width):
    cols = right.shape[2] // width

    def some(i, carry):
        ids = [tuple(order[k, i * UNROLL + u] for k in range(3)) for u in range(UNROLL)]
        for u, (s, _, _) in enumerate(ids):
            hi, lo = split(amp[pl.ds(pl.multiple_of(s * width, 8), width), 0:width])
            for at in (0, width):
                wide[u, 0:width, at : at + width] = hi
                wide[u, width : 2 * width, at : at + width] = lo
        for g in range(0, cols, PER):
            for u, (_, _, d) in enumerate(ids):
                span = slice(g * width, (g + PER) * width)
                r = lax.dot_general(wide[u], right[d, :, span], NN, preferred_element_type=F32)
                r = r[:width] + r[width:]
                for j in range(0, PER, 4):
                    at = [(j // 4 * 3 + k) * LANE for k in range(4)]
                    for q, v in enumerate(unpack(*(r[:, at[k] : at[k + 1]] for k in range(3)))):
                        hi, lo = split(v)
                        p = g + j + q
                        half[u, p * width : (p + 1) * width, 0:LANE] = hi
                        half[u, p * width : (p + 1) * width, LANE : 2 * LANE] = lo
        for u, (s, c, _) in enumerate(ids):
            o = lax.dot_general(left[c], half[u], NN, preferred_element_type=F32)
            o = o[:width, :LANE] + o[width:, :LANE] + o[:width, LANE:]
            acc[pl.ds(pl.multiple_of(s * width, 8), width), :] = o
        return carry

    lax.fori_loop(low, high, some, 0)


def scratch(cols, width, rows):
    return [
        pltpu.VMEM((max(rows, 1) * width, LANE), F32),
        pltpu.VMEM((UNROLL, 2 * width, 2 * width), BF),
        pltpu.VMEM((UNROLL, cols * width, 2 * LANE), BF),
    ]


def resident(x):
    return pltpu.with_memory_space_constraint(x, pltpu.SMEM if x.dtype == jnp.int32 else pltpu.VMEM)


def call(body, ins, keep, outs, width, rows, name, micros):
    vm, sm = pl.BlockSpec(memory_space=pltpu.VMEM), pl.BlockSpec(memory_space=pltpu.SMEM)
    arrays = [x for x, _ in ins]
    specs = [sm if scalars else vm for _, scalars in ins]
    shapes, aliases, olds = [], {}, 0
    for i, x in enumerate(keep):
        if isinstance(x, jax.Array):
            aliases[len(arrays)] = i
            arrays.append(resident(x))
            specs.append(sm if x.dtype == jnp.int32 else vm)
            olds += 1
            shapes.append((pltpu.SMEM if x.dtype == jnp.int32 else pltpu.VMEM)(x.shape, x.dtype))
        else:
            shapes.append(x)
    specs_out = [sm if x.dtype == jnp.int32 else vm for x in [*keep, *outs]]

    def kernel(*refs):
        refs = list(refs)
        given, refs = refs[: len(ins)], refs[len(ins) + olds :]
        states, refs = refs[: len(keep)], refs[len(keep) :]
        made, refs = refs[: len(outs)], refs[len(outs) :]
        body(given, states, made, *refs)

    results = pl.pallas_call(
        kernel,
        out_shape=shapes + list(outs),
        in_specs=specs,
        out_specs=specs_out,
        input_output_aliases=aliases,
        scratch_shapes=scratch(NAUX // 2, width, rows),
        compiler_params=pltpu.CompilerParams(vmem_limit_bytes=VMEM_BYTES),
        cost_estimate=pl.CostEstimate(flops=int(micros * 1e9), bytes_accessed=int(micros * 3e6), transcendentals=0),
        name=name,
    )(*arrays)
    return results[: len(keep)], results[len(keep) :]


def after(arrays, token):
    anywhere = pl.BlockSpec(memory_space=pl.ANY)
    return pl.pallas_call(
        lambda *refs: None,
        out_shape=[jax.ShapeDtypeStruct(x.shape, x.dtype) for x in arrays],
        in_specs=[anywhere] * (len(arrays) + 1),
        out_specs=[anywhere] * len(arrays),
        input_output_aliases={i: i for i in range(len(arrays))},
        compiler_params=pltpu.CompilerParams(vmem_limit_bytes=1 << 20),
        name="gate",
    )(*arrays, token)


def ring_order(mesh):
    devices = mesh.devices.reshape(mesh.shape["groups"], mesh.shape["pairs"])[0, ::2]
    count = len(devices)
    places = [tuple(getattr(d, "coords", None) or (i, 0, 0)) for i, d in enumerate(devices)]
    spread = [sorted({p[a] for p in places}) for a in range(len(places[0]))]
    varying = [a for a in range(len(spread)) if len(spread[a]) > 1]
    if len(varying) == 2 and min(len(spread[a]) for a in varying) == 2:
        short, long = sorted(varying, key=lambda a: len(spread[a]))
        up = sorted((i for i in range(count) if places[i][short] == spread[short][0]), key=lambda i: places[i][long])
        down = sorted((i for i in range(count) if places[i][short] != spread[short][0]), key=lambda i: -places[i][long])
        return up + down
    return list(range(count))


def shards(ring, amplitudes, block_list, factors):
    pair_rows, keep, cells = amplitudes.shape
    width = math.isqrt(cells)
    slots = pair_rows * keep
    held = factors.shape[0]
    chips = len(ring)
    steps = chips // 2
    parts = 2 if held % 8 == 0 else 1
    cut = held // parts
    per_block = NAUX // (2 * held)

    place = {c: i for i, c in enumerate(ring)}
    table = np.zeros((chips, chips + NB), np.int32)
    for c in range(chips):
        for j in range(chips):
            table[c, j] = ring[(place[c] + j) % chips]
        for j in range(chips):
            far = min(j, chips - j)
            b = table[c, j] // per_block
            table[c, chips + b] = max(table[c, chips + b], far)

    def shift(x, by):
        pairs = [
            (2 * ring[i] + core, 2 * ring[(i + by) % chips] + core) for i in range(chips) for core in range(2)
        ]
        return lax.ppermute(x, "pairs", pairs)

    def swap(x):
        return lax.ppermute(x, "pairs", [(i, i ^ 1) for i in range(2 * chips)])

    flat = amplitudes.reshape(slots, cells)
    labels = block_list.reshape(slots)
    row = lax.axis_index("pairs") // 2
    meta = lax.dynamic_slice(jnp.asarray(table), (row, 0), (1, chips + NB))

    up = [factors[i * cut : (i + 1) * cut] for i in range(parts)]
    down = list(up)
    arrivals = [[(x, 0, h * cut) for h, x in enumerate(up)]]
    cols = NAUX // 2
    tables = [pltpu.VMEM((NB, 2 * width, cols * width), BF)] * 2

    def fill(refs, pieces, meta_ref, tabs, mats):
        fill_table([(ref, o, f, held) for ref, (_, o, f) in zip(refs, pieces)], meta_ref, tabs, mats, width, per_block)

    def piece_ins(pieces):
        return [(x, False) for x, _, _ in pieces]

    def send(k, i):
        if len(arrivals) == k:
            arrivals.append([])
        if k < steps or i == 0:
            up[i] = shift(up[i], 1)
            arrivals[k].append((up[i], chips - k, i * cut))
        if k < steps or i == 1:
            down[i] = shift(down[i], -1)
            arrivals[k].append((down[i], k, i * cut))

    if 2 * slots <= GROUP:
        matrices = pltpu.VMEM(((2 * slots + 1) * width, LANE), F32)
        listed_shape = pltpu.SMEM((5, max(2 * slots + UNROLL, chips + NB)), jnp.int32)
        other_flat, other_labels = swap(flat), swap(labels)
        for i in range(parts):
            send(1, i)

        def prepare(given, states, made, mats, wide, half):
            meta_ref, own_l, other_l, own = given[:4]
            listed = states[4]
            total = order_slots([(other_l, slots), (own_l, 0)], meta_ref, chips, steps, listed)
            pad_order(listed, total, 2 * slots)
            for i in range(chips + NB):
                listed[4, i] = meta_ref[0, i]
            made[0][...] = jnp.zeros_like(made[0])
            load_matrices(own, states[2], 0, width)
            fill(given[4:], arrivals[0], meta_ref, states[:2], mats)

        state, (token,) = call(
            prepare,
            [(meta, True), (labels, True), (other_labels, True), (flat, False)] + piece_ins(arrivals[0]),
            tables + [matrices, matrices, listed_shape],
            [TOKEN],
            width,
            cut,
            "prepare",
            4,
        )

        def middle(listed, k):
            return (listed[3, k - 1] + listed[3, k] + 1) // 2

        for k in range(1, steps + 1):
            for i in range(parts if k < steps else 1):
                pieces = arrivals[k]
                if k < steps:
                    up[i], down[i] = after([up[i], down[i]], token)
                    pieces = [(up[i], chips - k, i * cut), (down[i], k, i * cut)]
                    send(k + 1, i)
                opening = [(other_flat, False)] if k == 1 and i == 0 else []
                closing = [jax.ShapeDtypeStruct(flat.shape, F32)] if k == steps else [TOKEN]

                def body(given, states, made, mats, wide, half, k=k, i=i, pieces=pieces, n=len(opening)):
                    listed = states[4]
                    fill(given[n:], pieces, listed.at[pl.ds(4, 1)], states[:2], mats)
                    if n:
                        load_matrices(given[0], states[2], slots, width)
                        states[3][...] = jnp.zeros_like(states[3])
                    bounds = [listed[3, k - 1], listed[3, k]]
                    if k == steps:
                        bounds = [listed[3, k - 1], listed[3, steps + 1]]
                    elif parts == 2 and k < steps - 1:
                        bounds = [listed[3, k - 1], middle(listed, k)]
                    if parts == 2 and i == 0 and k < steps:
                        bounds = [middle(listed, k - 1), listed[3, k - 1]] if k > 1 else None
                    if bounds is not None:
                        run_slots(*bounds, listed, *states[:4], wide, half, width)
                    if k == steps:
                        store_flat(states[3], slots, made[0], width)
                    else:
                        made[0][...] = jnp.zeros_like(made[0])

                state, (token,) = call(
                    body,
                    opening + piece_ins(pieces),
                    state,
                    closing,
                    width,
                    cut,
                    f"slots_step_{k}_{i}",
                    4,
                )
        back = swap(token)

        def last(given, states, made, mats, wide, half):
            listed = states[4]
            run_slots(listed[3, steps + 1], listed[3, steps], listed, *states[:4], wide, half, width)
            store_flat(states[3], 0, made[0], width)

        state, (own,) = call(last, [], state, [jax.ShapeDtypeStruct(flat.shape, F32)], width, 1, "slots_own", 2)
        result = own + back
    else:
        state = tables
        for k in range(1, steps + 1):
            for i in range(parts):
                send(k, i)
            pieces = (arrivals[0] if k == 1 else []) + arrivals[k]

            def body(given, states, made, mats, wide, half, pieces=pieces):
                fill(given[1:], pieces, given[0], states, mats)

            state, _ = call(body, [(meta, True)] + piece_ins(pieces), state, [], width, cut, f"table_step_{k}", 2)

        def group(given, states, made, mats, wide, half):
            meta_ref, names, rows = given
            result_ref, listed = made[:2]
            count = rows.shape[0]
            amp, acc = states[2:]
            total = order_slots([(names, 0)], meta_ref, chips, steps, listed)
            pad_order(listed, total, count)
            acc[...] = jnp.zeros_like(acc)
            load_matrices(rows, amp, 0, width)
            run_slots(0, listed[3, steps], listed, *states, wide, half, width)
            store_flat(acc, 0, result_ref, width)

        def grouped(rows, names):
            nonlocal state
            results = []
            for g in range(0, slots, GROUP):
                count = min(GROUP, slots - g)
                matrices = pltpu.VMEM(((count + 1) * width, LANE), F32)
                kept, made = call(
                    group,
                    [(meta, True), (names[g : g + count], True), (rows[g : g + count], False)],
                    [*state, matrices, matrices],
                    [
                        jax.ShapeDtypeStruct((count, cells), F32),
                        jax.ShapeDtypeStruct((4, count + max(UNROLL, steps + 2)), jnp.int32),
                    ],
                    width,
                    1,
                    f"slots_group_{g}",
                    20,
                )
                state = kept[:2]
                results.append(made[0])
            return jnp.concatenate(results) if len(results) > 1 else results[0]

        back = swap(grouped(swap(flat), swap(labels)))
        result = grouped(flat, labels) + back
    return result.reshape(pair_rows, keep, cells)


def solution(mesh):
    return jax.shard_map(
        functools.partial(shards, ring_order(mesh)),
        mesh=mesh,
        in_specs=(
            P(("groups", "pairs"), None, None),
            P(("groups", "pairs"), None),
            P(("groups", "pairs"), None),
        ),
        out_specs=P(("groups", "pairs"), None, None),
        check_vma=False,
    )
```

```python
import functools
import math

import jax
import jax.numpy as jnp
import numpy as np
from jax import lax
from jax.experimental import pallas as pl
from jax.experimental.pallas import tpu as pltpu
from jax.sharding import PartitionSpec as P

NB = 8
NAUX = 32
LANE = 128
UNROLL = 4
WIDE = 8
PER = 8
GROUP = 64
BF = jnp.bfloat16
F32 = jnp.float32
NN = (((1,), (0,)), ((), ()))
VMEM_BYTES = 22 << 20
TOKEN = jax.ShapeDtypeStruct((8, LANE), F32)


def split(x):
    hi = x.astype(BF)
    return hi, (x - hi.astype(F32)).astype(BF)


def unpack(y0, y1, y2):
    lane = lax.broadcasted_iota(jnp.int32, y0.shape, 1)
    v1, v2 = jnp.where(lane >= 96, y0, y1), jnp.where(lane >= 64, y1, y2)
    return y0, pltpu.roll(v1, 32, 1), pltpu.roll(v2, 64, 1), pltpu.roll(y2, 96, 1)


def unflatten(read, write, width):
    for m in range(width // 4):
        for r, v in enumerate(unpack(*(read(3 * m + j) for j in range(3)))):
            write(4 * m + r, v)


def pack(v0, v1, v2, v3):
    lane = lax.broadcasted_iota(jnp.int32, v0.shape, 1)
    v1, v2, v3 = pltpu.roll(v1, 96, 1), pltpu.roll(v2, 64, 1), pltpu.roll(v3, 32, 1)
    return jnp.where(lane < 96, v0, v1), jnp.where(lane < 64, v1, v2), jnp.where(lane < 32, v2, v3)


def flatten(read, write, width):
    for m in range(width // 4):
        for j, y in enumerate(pack(*(read(4 * m + r) for r in range(4)))):
            write(3 * m + j, y)


def load_matrices(flat, mats, first, width):
    rows = flat.shape[0]
    step = min(8, rows)

    def group(g, carry):
        at = pl.multiple_of(g * step, step)
        base = pl.multiple_of((first + g * step) * width, 8)

        def read(j):
            return flat[pl.ds(at, step), j * LANE : (j + 1) * LANE]

        def write(e, v):
            mats[pl.ds(base + e, step, stride=width), :] = v

        unflatten(read, write, width)
        return carry

    lax.fori_loop(0, rows // step, group, 0)


def store_flat(mats, first, out, width):
    rows = out.shape[0]
    step = min(8, rows)

    def group(g, carry):
        at = pl.multiple_of(g * step, step)
        base = pl.multiple_of((first + g * step) * width, 8)

        def read(e):
            return mats[pl.ds(base + e, step, stride=width), :]

        def write(j, v):
            out[pl.ds(at, step), j * LANE : (j + 1) * LANE] = v

        flatten(read, write, width)
        return carry

    lax.fori_loop(0, rows // step, group, 0)


def fill_table(pieces, meta, tabs, mats, width, per_block):
    right, left = tabs
    for flat, offset, first, held in pieces:
        rows = flat.shape[0]
        load_matrices(flat, mats, 0, width)
        chip = meta[0, offset]
        block = chip // per_block
        lead = (chip % per_block) * held + first
        for i in range(0, rows, 4):
            four = [mats[(i + r) * width : (i + r + 1) * width, :] for r in range(4)]
            blank = jnp.zeros((width, LANE - width), F32)
            turned = [jnp.concatenate([x.T[:width], blank], axis=1) for x in four]
            for table, matrices in ((left, four), (right, turned)):
                for j, y in enumerate(pack(*matrices)):
                    hi, lo = split(y)
                    at = pl.multiple_of(((lead + i) // 4 * 3 + j) * LANE, LANE)
                    table[block, 0:width, pl.ds(at, LANE)] = hi
                    table[block, width : 2 * width, pl.ds(at, LANE)] = lo


def order_slots(labels, meta, chips, steps, order):
    for r in range(steps + 2):
        order[3, r] = 0

    def ready_of(v):
        c, d = jnp.maximum(v, 0) >> 3, jnp.maximum(v, 0) & 7
        ready = jnp.maximum(jnp.maximum(meta[0, chips + c], meta[0, chips + d]), 1)
        return jnp.where(v >= 0, ready, steps + 1), c, d

    def tally(ref):
        for row in range(ref.shape[0]):

            def one(i, carry, row=row):
                ready, _, _ = ready_of(ref[row, i])
                order[3, ready] = order[3, ready] + 1
                return carry

            lax.fori_loop(0, ref.shape[1], one, 0, unroll=8)

    tally(labels[0][0])
    early = order[3, steps]
    for ref, _ in labels[1:]:
        tally(ref)
    early = jnp.maximum(early, order[3, steps] - early)
    total = 0
    for r in range(1, steps + 1):
        count = order[3, r]
        order[3, r] = total
        total = total + count
    order[3, steps + 1] = total
    early = early + order[3, steps]

    def put(ref, first):
        for row in range(ref.shape[0]):

            def one(i, carry, row=row):
                ready, c, d = ready_of(ref[row, i])
                n = order[3, ready]
                order[0, n] = first + row * ref.shape[1] + i
                order[1, n] = c
                order[2, n] = d
                order[3, ready] = n + 1
                return carry

            lax.fori_loop(0, ref.shape[1], one, 0, unroll=8)

    for ref, first in labels:
        put(ref, first)
    for r in range(1, steps):
        order[3, r] = order[3, r] // UNROLL
    order[3, 0] = 0
    order[3, steps] = (total + UNROLL - 1) // UNROLL
    order[3, steps + 1] = (early + UNROLL - 1) // UNROLL
    return total


def pad_order(order, total, dummy):
    for u in range(UNROLL - 1):
        order[0, total + u] = dummy
        order[1, total + u] = 0
        order[2, total + u] = 0


def run_slots(low, high, order, right, left, amp, acc, wide, half, width, functions=None):
    first, stop = functions or (0, right.shape[2] // width)

    def some(base, count):
        ids = [tuple(order[k, base + u] for k in range(3)) for u in range(count)]
        for u, (s, _, _) in enumerate(ids):
            hi, lo = split(amp[pl.ds(pl.multiple_of(s * width, 8), width), 0:width])
            for at in (0, width):
                wide[u, 0:width, at : at + width] = hi
                wide[u, width : 2 * width, at : at + width] = lo
        for g in range(first, stop, PER):
            for u, (_, _, d) in enumerate(ids):
                span = slice(g * width, (g + PER) * width)
                r = lax.dot_general(wide[u], right[d, :, span], NN, preferred_element_type=F32)
                r = r[:width] + r[width:]
                for j in range(0, PER, 4):
                    at = [(j // 4 * 3 + k) * LANE for k in range(4)]
                    for q, v in enumerate(unpack(*(r[:, at[k] : at[k + 1]] for k in range(3)))):
                        hi, lo = split(v)
                        p = g + j + q
                        half[u, p * width : (p + 1) * width, 0:LANE] = hi
                        half[u, p * width : (p + 1) * width, LANE : 2 * LANE] = lo
        for u, (s, c, _) in enumerate(ids):
            span = slice(first * width, stop * width)
            o = lax.dot_general(left[c, :, span], half[u, span, :], NN, preferred_element_type=F32)
            o = o[:width, :LANE] + o[width:, :LANE] + o[:width, LANE:]
            at = pl.ds(pl.multiple_of(s * width, 8), width)
            acc[at, :] = o if first == 0 else acc[at, :] + o

    def many(i, carry):
        some(low * UNROLL + i * WIDE, WIDE)
        return carry

    def few(i, carry):
        some((high - 1) * UNROLL, UNROLL)
        return carry

    twos = (high - low) // (WIDE // UNROLL)
    lax.fori_loop(0, twos, many, 0)
    lax.fori_loop(0, high - low - twos * (WIDE // UNROLL), few, 0)


def scratch(cols, width, rows):
    return [
        pltpu.VMEM((max(rows, 1) * width, LANE), F32),
        pltpu.VMEM((WIDE, 2 * width, 2 * width), BF),
        pltpu.VMEM((WIDE, cols * width, 2 * LANE), BF),
    ]


def resident(x):
    return pltpu.with_memory_space_constraint(x, pltpu.SMEM if x.dtype == jnp.int32 else pltpu.VMEM)


def call(body, ins, keep, outs, width, rows, name, micros):
    vm, sm = pl.BlockSpec(memory_space=pltpu.VMEM), pl.BlockSpec(memory_space=pltpu.SMEM)
    arrays = [x for x, _ in ins]
    specs = [sm if scalars else vm for _, scalars in ins]
    shapes, aliases, olds = [], {}, 0
    for i, x in enumerate(keep):
        if isinstance(x, jax.Array):
            aliases[len(arrays)] = i
            arrays.append(resident(x))
            specs.append(sm if x.dtype == jnp.int32 else vm)
            olds += 1
            shapes.append((pltpu.SMEM if x.dtype == jnp.int32 else pltpu.VMEM)(x.shape, x.dtype))
        else:
            shapes.append(x)
    specs_out = [sm if x.dtype == jnp.int32 else vm for x in [*keep, *outs]]

    def kernel(*refs):
        refs = list(refs)
        given, refs = refs[: len(ins)], refs[len(ins) + olds :]
        states, refs = refs[: len(keep)], refs[len(keep) :]
        made, refs = refs[: len(outs)], refs[len(outs) :]
        body(given, states, made, *refs)

    results = pl.pallas_call(
        kernel,
        out_shape=shapes + list(outs),
        in_specs=specs,
        out_specs=specs_out,
        input_output_aliases=aliases,
        scratch_shapes=scratch(NAUX // 2, width, rows),
        compiler_params=pltpu.CompilerParams(vmem_limit_bytes=VMEM_BYTES),
        cost_estimate=pl.CostEstimate(flops=int(micros * 1e9), bytes_accessed=int(micros * 3e6), transcendentals=0),
        name=name,
    )(*arrays)
    return results[: len(keep)], results[len(keep) :]


def after(arrays, token):
    anywhere = pl.BlockSpec(memory_space=pl.ANY)
    return pl.pallas_call(
        lambda *refs: None,
        out_shape=[jax.ShapeDtypeStruct(x.shape, x.dtype) for x in arrays],
        in_specs=[anywhere] * (len(arrays) + 1),
        out_specs=[anywhere] * len(arrays),
        input_output_aliases={i: i for i in range(len(arrays))},
        compiler_params=pltpu.CompilerParams(vmem_limit_bytes=1 << 20),
        name="gate",
    )(*arrays, token)


def ring_order(mesh):
    devices = mesh.devices.reshape(mesh.shape["groups"], mesh.shape["pairs"])[0, ::2]
    count = len(devices)
    places = [tuple(getattr(d, "coords", None) or (i, 0, 0)) for i, d in enumerate(devices)]
    spread = [sorted({p[a] for p in places}) for a in range(len(places[0]))]
    varying = [a for a in range(len(spread)) if len(spread[a]) > 1]
    if len(varying) == 2 and min(len(spread[a]) for a in varying) == 2:
        short, long = sorted(varying, key=lambda a: len(spread[a]))
        up = sorted((i for i in range(count) if places[i][short] == spread[short][0]), key=lambda i: places[i][long])
        down = sorted((i for i in range(count) if places[i][short] != spread[short][0]), key=lambda i: -places[i][long])
        return up + down
    return list(range(count))


def shards(ring, amplitudes, block_list, factors):
    pair_rows, keep, cells = amplitudes.shape
    width = math.isqrt(cells)
    slots = pair_rows * keep
    held = factors.shape[0]
    chips = len(ring)
    steps = chips // 2
    per_block = NAUX // (2 * held)
    parts = 2 if per_block == 1 else 1
    cut = held // parts

    place = {c: i for i, c in enumerate(ring)}
    table = np.zeros((chips, chips + NB), np.int32)
    for c in range(chips):
        for j in range(chips):
            table[c, j] = ring[(place[c] + j) % chips]
        for j in range(chips):
            far = min(j, chips - j)
            b = table[c, j] // per_block
            table[c, chips + b] = max(table[c, chips + b], far)

    def shift(x, by):
        pairs = [
            (2 * ring[i] + core, 2 * ring[(i + by) % chips] + core) for i in range(chips) for core in range(2)
        ]
        return lax.ppermute(x, "pairs", pairs)

    def swap(x):
        return lax.ppermute(x, "pairs", [(i, i ^ 1) for i in range(2 * chips)])

    flat = amplitudes.reshape(slots, cells)
    labels = block_list
    row = lax.axis_index("pairs") // 2
    meta = lax.dynamic_slice(jnp.asarray(table), (row, 0), (1, chips + NB))

    up = [factors[i * cut : (i + 1) * cut] for i in range(parts)]
    down = list(up)
    arrivals = [[(x, 0, h * cut) for h, x in enumerate(up)]]
    cols = NAUX // 2
    tables = [pltpu.VMEM((NB, 2 * width, cols * width), BF)] * 2

    def fill(refs, pieces, meta_ref, tabs, mats):
        fill_table([(ref, o, f, held) for ref, (_, o, f) in zip(refs, pieces)], meta_ref, tabs, mats, width, per_block)

    def piece_ins(pieces):
        return [(x, False) for x, _, _ in pieces]

    def send(k, i):
        if len(arrivals) == k:
            arrivals.append([])
        if k < steps or i == 0:
            up[i] = shift(up[i], 1)
            arrivals[k].append((up[i], chips - k, i * cut))
        if k < steps or i == 1:
            down[i] = shift(down[i], -1)
            arrivals[k].append((down[i], k, i * cut))

    if 2 * slots <= GROUP:
        matrices = pltpu.VMEM(((2 * slots + 1) * width, LANE), F32)
        listed_shape = pltpu.SMEM((5, max(2 * slots + UNROLL, chips + NB)), jnp.int32)
        other_flat, other_labels = swap(flat), swap(labels)
        for i in range(parts):
            send(1, i)

        def arrange(given, states, made, mats, wide, half):
            meta_ref, own_l, other_l = given
            (listed,) = states
            total = order_slots([(other_l, slots), (own_l, 0)], meta_ref, chips, steps, listed)
            pad_order(listed, total, 2 * slots)
            for i in range(chips + NB):
                listed[4, i] = meta_ref[0, i]

        (listed,), _ = call(
            arrange, [(meta, True), (labels, True), (other_labels, True)], [listed_shape], [], width, 1, "arrange", 2
        )

        def prepare(given, states, made, mats, wide, half):
            load_matrices(given[0], states[2], 0, width)
            load_matrices(given[1], states[2], slots, width)
            states[3][...] = jnp.zeros_like(states[3])
            made[0][...] = jnp.zeros_like(made[0])
            fill(given[2:], arrivals[0], states[4].at[pl.ds(4, 1)], states[:2], mats)

        state, (token,) = call(
            prepare,
            [(flat, False), (other_flat, False)] + piece_ins(arrivals[0]),
            tables + [matrices, matrices, listed],
            [TOKEN],
            width,
            cut,
            "prepare",
            4,
        )

        def part_of(i):
            return (i * cut, (i + 1) * cut) if parts == 2 else None

        for k in range(1, steps + 1):
            for i in range(parts):
                if k < steps:
                    up[i], down[i] = after([up[i], down[i]], token)
                    pieces = [(up[i], chips - k, i * cut), (down[i], k, i * cut)]
                    send(k + 1, i)
                else:
                    pieces = arrivals[k][i : i + 1]
                final = k == steps and i == parts - 1
                closing = [jax.ShapeDtypeStruct(flat.shape, F32)] if final else [TOKEN]

                def body(given, states, made, mats, wide, half, k=k, i=i, pieces=pieces, final=final):
                    listed = states[4]
                    fill(given, pieces, listed.at[pl.ds(4, 1)], states[:2], mats)
                    high = listed[3, steps + 1 if final else k]
                    run_slots(listed[3, k - 1], high, listed, *states[:4], wide, half, width, part_of(i))
                    if final:
                        store_flat(states[3], slots, made[0], width)
                    else:
                        made[0][...] = jnp.zeros_like(made[0])

                state, (token,) = call(
                    body,
                    piece_ins(pieces),
                    state,
                    closing,
                    width,
                    cut,
                    f"slots_step_{k}_{i}",
                    4,
                )
        back = swap(token)

        def last(given, states, made, mats, wide, half):
            listed = states[4]
            run_slots(listed[3, steps + 1], listed[3, steps], listed, *states[:4], wide, half, width, part_of(parts - 1))
            store_flat(states[3], 0, made[0], width)

        state, (own,) = call(last, [], state, [jax.ShapeDtypeStruct(flat.shape, F32)], width, 1, "slots_own", 2)
        result = own + back
    else:
        state = tables
        for k in range(1, steps + 1):
            for i in range(parts):
                send(k, i)
            pieces = (arrivals[0] if k == 1 else []) + arrivals[k]

            def body(given, states, made, mats, wide, half, pieces=pieces):
                fill(given[1:], pieces, given[0], states, mats)

            state, _ = call(body, [(meta, True)] + piece_ins(pieces), state, [], width, cut, f"table_step_{k}", 2)

        def group(given, states, made, mats, wide, half):
            meta_ref, names, rows = given
            result_ref, listed = made[:2]
            count = rows.shape[0]
            amp, acc = states[2:]
            total = order_slots([(names, 0)], meta_ref, chips, steps, listed)
            pad_order(listed, total, count)
            acc[...] = jnp.zeros_like(acc)
            load_matrices(rows, amp, 0, width)
            run_slots(0, listed[3, steps], listed, *states, wide, half, width)
            store_flat(acc, 0, result_ref, width)

        def grouped(rows, names):
            nonlocal state
            results = []
            for g in range(0, slots, GROUP):
                count = min(GROUP, slots - g)
                matrices = pltpu.VMEM(((count + 1) * width, LANE), F32)
                kept, made = call(
                    group,
                    [(meta, True), (names[g // keep : (g + count) // keep], True), (rows[g : g + count], False)],
                    [*state, matrices, matrices],
                    [
                        jax.ShapeDtypeStruct((count, cells), F32),
                        jax.ShapeDtypeStruct((4, count + max(UNROLL, steps + 2)), jnp.int32),
                    ],
                    width,
                    1,
                    f"slots_group_{g}",
                    20,
                )
                state = kept[:2]
                results.append(made[0])
            return jnp.concatenate(results) if len(results) > 1 else results[0]

        back = swap(grouped(swap(flat), swap(labels)))
        result = grouped(flat, labels) + back
    return result.reshape(pair_rows, keep, cells)


def solution(mesh):
    return jax.shard_map(
        functools.partial(shards, ring_order(mesh)),
        mesh=mesh,
        in_specs=(
            P(("groups", "pairs"), None, None),
            P(("groups", "pairs"), None),
            P(("groups", "pairs"), None),
        ),
        out_specs=P(("groups", "pairs"), None, None),
        check_vma=False,
    )
```

```python
import functools
import math

import jax
import jax.numpy as jnp
import numpy as np
from jax import lax
from jax.experimental import pallas as pl
from jax.experimental.pallas import tpu as pltpu
from jax.sharding import PartitionSpec as P

NB = 8
NAUX = 32
LANE = 128
UNROLL = 4
WIDE = 8
PER = 8
GROUP = 64
BF = jnp.bfloat16
F32 = jnp.float32
NN = (((1,), (0,)), ((), ()))
VMEM_BYTES = 22 << 20
TOKEN = jax.ShapeDtypeStruct((8, LANE), F32)


def pitch(width):
    return width + 8 if width % 16 == 0 else width


def split(x):
    hi = x.astype(BF)
    return hi, (x - hi.astype(F32)).astype(BF)


def unpack(y0, y1, y2):
    lane = lax.broadcasted_iota(jnp.int32, y0.shape, 1)
    v1, v2 = jnp.where(lane >= 96, y0, y1), jnp.where(lane >= 64, y1, y2)
    return y0, pltpu.roll(v1, 32, 1), pltpu.roll(v2, 64, 1), pltpu.roll(y2, 96, 1)


def unflatten(read, write, width):
    for m in range(width // 4):
        for r, v in enumerate(unpack(*(read(3 * m + j) for j in range(3)))):
            write(4 * m + r, v)


def pack(v0, v1, v2, v3):
    lane = lax.broadcasted_iota(jnp.int32, v0.shape, 1)
    v1, v2, v3 = pltpu.roll(v1, 96, 1), pltpu.roll(v2, 64, 1), pltpu.roll(v3, 32, 1)
    return jnp.where(lane < 96, v0, v1), jnp.where(lane < 64, v1, v2), jnp.where(lane < 32, v2, v3)


def flatten(read, write, width):
    for m in range(width // 4):
        for j, y in enumerate(pack(*(read(4 * m + r) for r in range(4)))):
            write(3 * m + j, y)


def load_matrices(flat, mats, first, width):
    rows = flat.shape[0]
    step = min(8, rows)

    def group(g, carry):
        at = pl.multiple_of(g * step, step)
        base = pl.multiple_of((first + g * step) * pitch(width), 8)

        def read(j):
            return flat[pl.ds(at, step), j * LANE : (j + 1) * LANE]

        def write(e, v):
            mats[pl.ds(base + e, step, stride=pitch(width)), :] = v

        unflatten(read, write, width)
        return carry

    lax.fori_loop(0, rows // step, group, 0)


def store_flat(mats, first, out, width):
    rows = out.shape[0]
    step = min(8, rows)

    def group(g, carry):
        at = pl.multiple_of(g * step, step)
        base = pl.multiple_of((first + g * step) * pitch(width), 8)

        def read(e):
            return mats[pl.ds(base + e, step, stride=pitch(width)), :]

        def write(j, v):
            out[pl.ds(at, step), j * LANE : (j + 1) * LANE] = v

        flatten(read, write, width)
        return carry

    lax.fori_loop(0, rows // step, group, 0)


def fill_table(pieces, meta, tabs, mats, width, per_block):
    right, left = tabs
    for flat, offset, first, held in pieces:
        rows = flat.shape[0]
        load_matrices(flat, mats, 0, width)
        chip = meta[0, offset]
        block = chip // per_block
        lead = (chip % per_block) * held + first
        for i in range(0, rows, 4):
            four = [mats[(i + r) * pitch(width) : (i + r) * pitch(width) + width, :] for r in range(4)]
            blank = jnp.zeros((width, LANE - width), F32)
            turned = [jnp.concatenate([x.T[:width], blank], axis=1) for x in four]
            for table, matrices in ((left, four), (right, turned)):
                for j, y in enumerate(pack(*matrices)):
                    hi, lo = split(y)
                    at = pl.multiple_of(((lead + i) // 4 * 3 + j) * LANE, LANE)
                    table[block, 0:width, pl.ds(at, LANE)] = hi
                    table[block, width : 2 * width, pl.ds(at, LANE)] = lo


def order_slots(labels, meta, chips, steps, order):
    for r in range(steps + 2):
        order[3, r] = 0

    def ready_of(v):
        c, d = jnp.maximum(v, 0) >> 3, jnp.maximum(v, 0) & 7
        x, y = meta[0, chips + c], meta[0, chips + d]
        last = jnp.maximum(x, y)
        both = ((x >> 1) == (y >> 1)) & (x != y)
        ready = jnp.maximum((last >> 1) + jnp.where(both, 1, 0), 1)
        return jnp.where(v >= 0, ready, steps + 1), c, d, last & 1

    def tally(ref):
        for row in range(ref.shape[0]):

            def one(i, carry, row=row):
                ready = ready_of(ref[row, i])[0]
                order[3, ready] = order[3, ready] + 1
                return carry

            lax.fori_loop(0, ref.shape[1], one, 0, unroll=8)

    tally(labels[0][0])
    early = order[3, steps]
    for ref, _ in labels[1:]:
        tally(ref)
    early = jnp.maximum(early, order[3, steps] - early)
    total = 0
    for r in range(1, steps + 1):
        count = order[3, r]
        order[3, r] = total
        total = total + count
    order[3, steps + 1] = total
    early = early + order[3, steps]

    def put(ref, first):
        for row in range(ref.shape[0]):

            def one(i, carry, row=row):
                ready, c, d, part = ready_of(ref[row, i])
                n = order[3, ready]
                order[0, n] = first + row * ref.shape[1] + i
                order[1, n] = c
                order[2, n] = d
                order[4, n] = part
                order[3, ready] = n + 1
                return carry

            lax.fori_loop(0, ref.shape[1], one, 0, unroll=8)

    for ref, first in labels:
        put(ref, first)
    for r in range(1, steps):
        order[3, r] = order[3, r] // UNROLL
    order[3, 0] = 0
    order[3, steps] = (total + UNROLL - 1) // UNROLL
    order[3, steps + 1] = (early + UNROLL - 1) // UNROLL
    return total


def pad_order(order, total, dummy):
    for u in range(UNROLL - 1):
        order[0, total + u] = dummy
        order[1, total + u] = 0
        order[2, total + u] = 0
        order[4, total + u] = 0


def run_slots(low, high, order, right, left, amp, acc, wide, half, width, phase=None):
    cols = right.shape[2] // width
    if phase is not None:
        cols = cols // 2

    def some(base, count):
        ids = [tuple(order[k, base + u] for k in range(3)) for u in range(count)]
        starts = [0] * count
        if phase is not None:
            parts = [order[4, base + u] for u in range(count)]
            starts = [pl.multiple_of((p if phase == 0 else 1 - p) * (cols * width), LANE) for p in parts]
        for u, (s, _, _) in enumerate(ids):
            hi, lo = split(amp[pl.ds(pl.multiple_of(s * pitch(width), 8), width), 0:width])
            for at in (0, width):
                wide[u, 0:width, at : at + width] = hi
                wide[u, width : 2 * width, at : at + width] = lo
        for g in range(0, cols, PER):
            for u, (_, _, d) in enumerate(ids):
                span = pl.ds(starts[u] + g * width, PER * width)
                r = lax.dot_general(wide[u], right[d, :, span], NN, preferred_element_type=F32)
                r = r[:width] + r[width:]
                for j in range(0, PER, 4):
                    at = [(j // 4 * 3 + k) * LANE for k in range(4)]
                    for q, v in enumerate(unpack(*(r[:, at[k] : at[k + 1]] for k in range(3)))):
                        hi, lo = split(v)
                        p = g + j + q
                        half[u, p * width : (p + 1) * width, 0:LANE] = hi
                        half[u, p * width : (p + 1) * width, LANE : 2 * LANE] = lo
        for u, (s, c, _) in enumerate(ids):
            span = pl.ds(starts[u], cols * width)
            o = lax.dot_general(left[c, :, span], half[u, 0 : cols * width, :], NN, preferred_element_type=F32)
            o = o[:width, :LANE] + o[width:, :LANE] + o[:width, LANE:]
            at = pl.ds(pl.multiple_of(s * pitch(width), 8), width)
            acc[at, :] = acc[at, :] + o if phase == 1 else o

    def many(i, carry):
        some(low * UNROLL + i * WIDE, WIDE)
        return carry

    def few(i, carry):
        some((high - 1) * UNROLL, UNROLL)
        return carry

    twos = (high - low) // (WIDE // UNROLL)
    lax.fori_loop(0, twos, many, 0)
    lax.fori_loop(0, high - low - twos * (WIDE // UNROLL), few, 0)


def scratch(cols, width, rows):
    return [
        pltpu.VMEM((max(rows, 1) * pitch(width), LANE), F32),
        pltpu.VMEM((WIDE, 2 * width, 2 * width), BF),
        pltpu.VMEM((WIDE, cols * width, 2 * LANE), BF),
    ]


def resident(x):
    return pltpu.with_memory_space_constraint(x, pltpu.SMEM if x.dtype == jnp.int32 else pltpu.VMEM)


def call(body, ins, keep, outs, width, rows, name, micros):
    vm, sm = pl.BlockSpec(memory_space=pltpu.VMEM), pl.BlockSpec(memory_space=pltpu.SMEM)
    arrays = [x for x, _ in ins]
    specs = [sm if scalars else vm for _, scalars in ins]
    shapes, aliases, olds = [], {}, 0
    for i, x in enumerate(keep):
        if isinstance(x, jax.Array):
            aliases[len(arrays)] = i
            arrays.append(resident(x))
            specs.append(sm if x.dtype == jnp.int32 else vm)
            olds += 1
            shapes.append((pltpu.SMEM if x.dtype == jnp.int32 else pltpu.VMEM)(x.shape, x.dtype))
        else:
            shapes.append(x)
    specs_out = [sm if x.dtype == jnp.int32 else vm for x in [*keep, *outs]]

    def kernel(*refs):
        refs = list(refs)
        given, refs = refs[: len(ins)], refs[len(ins) + olds :]
        states, refs = refs[: len(keep)], refs[len(keep) :]
        made, refs = refs[: len(outs)], refs[len(outs) :]
        body(given, states, made, *refs)

    results = pl.pallas_call(
        kernel,
        out_shape=shapes + list(outs),
        in_specs=specs,
        out_specs=specs_out,
        input_output_aliases=aliases,
        scratch_shapes=scratch(NAUX // 2, width, rows),
        compiler_params=pltpu.CompilerParams(vmem_limit_bytes=VMEM_BYTES),
        cost_estimate=pl.CostEstimate(flops=int(micros * 1e9), bytes_accessed=int(micros * 3e6), transcendentals=0),
        name=name,
    )(*arrays)
    return results[: len(keep)], results[len(keep) :]


def after(arrays, token):
    anywhere = pl.BlockSpec(memory_space=pl.ANY)
    return pl.pallas_call(
        lambda *refs: None,
        out_shape=[jax.ShapeDtypeStruct(x.shape, x.dtype) for x in arrays],
        in_specs=[anywhere] * (len(arrays) + 1),
        out_specs=[anywhere] * len(arrays),
        input_output_aliases={i: i for i in range(len(arrays))},
        compiler_params=pltpu.CompilerParams(vmem_limit_bytes=1 << 20),
        name="gate",
    )(*arrays, token)


def copy_rows(x, parts, token):
    rows = x.shape[0] // parts

    def kernel(whole, _, *refs):
        outs, sems = refs[:parts], refs[parts]
        copies = [
            pltpu.make_async_copy(whole.at[pl.ds(i * rows, rows)], outs[i], sems.at[i]) for i in range(parts)
        ]
        for c in copies:
            c.start()
        for c in copies:
            c.wait()

    return pl.pallas_call(
        kernel,
        out_shape=[pltpu.VMEM((rows, x.shape[1]), x.dtype)] * parts,
        in_specs=[pl.BlockSpec(memory_space=pl.ANY)] * 2,
        out_specs=[pl.BlockSpec(memory_space=pltpu.VMEM)] * parts,
        scratch_shapes=[pltpu.SemaphoreType.DMA((parts,))],
        compiler_params=pltpu.CompilerParams(vmem_limit_bytes=1 << 20),
        name="copy_rows",
    )(x, token)


def ring_order(mesh):
    devices = mesh.devices.reshape(mesh.shape["groups"], mesh.shape["pairs"])[0, ::2]
    count = len(devices)
    places = [tuple(getattr(d, "coords", None) or (i, 0, 0)) for i, d in enumerate(devices)]
    spread = [sorted({p[a] for p in places}) for a in range(len(places[0]))]
    varying = [a for a in range(len(spread)) if len(spread[a]) > 1]
    if len(varying) == 2 and min(len(spread[a]) for a in varying) == 2:
        short, long = sorted(varying, key=lambda a: len(spread[a]))
        up = sorted((i for i in range(count) if places[i][short] == spread[short][0]), key=lambda i: places[i][long])
        down = sorted((i for i in range(count) if places[i][short] != spread[short][0]), key=lambda i: -places[i][long])
        return up + down
    return list(range(count))


def shards(ring, amplitudes, block_list, factors):
    pair_rows, keep, cells = amplitudes.shape
    width = math.isqrt(cells)
    slots = pair_rows * keep
    held = factors.shape[0]
    chips = len(ring)
    steps = chips // 2
    per_block = NAUX // (2 * held)
    parts = 2 if per_block == 1 else 1
    cut = held // parts

    place = {c: i for i, c in enumerate(ring)}
    table = np.zeros((chips, chips + NB), np.int32)
    for c in range(chips):
        for j in range(chips):
            table[c, j] = ring[(place[c] + j) % chips]
        for j in range(chips):
            far = min(j, chips - j)
            b = table[c, j] // per_block
            table[c, chips + b] = max(table[c, chips + b], 2 * far + (0 < j < chips - j))

    def shift(x, by):
        pairs = [
            (2 * ring[i] + core, 2 * ring[(i + by) % chips] + core) for i in range(chips) for core in range(2)
        ]
        return lax.ppermute(x, "pairs", pairs)

    def swap(x):
        return lax.ppermute(x, "pairs", [(i, i ^ 1) for i in range(2 * chips)])

    flat = amplitudes.reshape(slots, cells)
    labels = block_list
    row = lax.axis_index("pairs") // 2
    meta = lax.dynamic_slice(jnp.asarray(table), (row, 0), (1, chips + NB))

    up = [factors[i * cut : (i + 1) * cut] for i in range(parts)]
    down = list(up)
    arrivals = [[(x, 0, h * cut) for h, x in enumerate(up)]]
    cols = NAUX // 2
    tables = [pltpu.VMEM((NB, 2 * width, cols * width), BF)] * 2

    def fill(refs, pieces, meta_ref, tabs, mats):
        fill_table([(ref, o, f, held) for ref, (_, o, f) in zip(refs, pieces)], meta_ref, tabs, mats, width, per_block)

    def piece_ins(pieces):
        return [(x, False) for x, _, _ in pieces]

    def send(k, i):
        if len(arrivals) == k:
            arrivals.append([])
        o = parts - 1 - i
        if k < steps or i == 0:
            up[i] = shift(up[i], 1)
            arrivals[k].append((up[i], chips - k, i * cut))
        if k < steps or (i == 0 and parts == 2):
            down[o] = shift(down[o], -1)
            arrivals[k].append((down[o], k, o * cut))

    if 2 * slots <= GROUP:
        matrices = pltpu.VMEM(((2 * slots + 1) * pitch(width), LANE), F32)
        listed_shape = pltpu.SMEM((6, max(2 * slots + UNROLL, chips + NB)), jnp.int32)
        other_flat, other_labels = swap(flat), swap(labels)
        send(1, 0)
        if parts == 2:
            down[0], up[1] = copy_rows(factors, parts, other_labels)
            send(1, 1)

        def arrange(given, states, made, mats, wide, half):
            meta_ref, own_l, other_l = given
            (listed,) = states
            total = order_slots([(other_l, slots), (own_l, 0)], meta_ref, chips, steps, listed)
            pad_order(listed, total, 2 * slots)
            for i in range(chips + NB):
                listed[5, i] = meta_ref[0, i]

        (listed,), _ = call(
            arrange, [(meta, True), (labels, True), (other_labels, True)], [listed_shape], [], width, 1, "arrange", 2
        )

        def prepare(given, states, made, mats, wide, half):
            load_matrices(given[0], states[2], 0, width)
            load_matrices(given[1], states[2], slots, width)
            states[3][...] = jnp.zeros_like(states[3])
            made[0][...] = jnp.zeros_like(made[0])
            fill(given[2:], arrivals[0], states[4].at[pl.ds(5, 1)], states[:2], mats)

        state, (token,) = call(
            prepare,
            [(flat, False), (other_flat, False)] + piece_ins(arrivals[0]),
            tables + [matrices, matrices, listed],
            [TOKEN],
            width,
            cut,
            "prepare",
            4,
        )

        for k in range(1, steps + 1):
            final = k == steps
            for i in range(1 if final else parts):
                o = parts - 1 - i
                pieces = arrivals[k]
                if not final:
                    if k < steps - 1 or i == 0:
                        up[i], down[o] = after([up[i], down[o]], token)
                    pieces = [(up[i], chips - k, i * cut), (down[o], k, o * cut)]
                    send(k + 1, i)
                tied = k < steps - 1
                closing = [jax.ShapeDtypeStruct(flat.shape, F32)] if final else [TOKEN] * tied

                def body(given, states, made, mats, wide, half, k=k, i=i, pieces=pieces, final=final, tied=tied):
                    listed = states[4]
                    fill(given, pieces, listed.at[pl.ds(5, 1)], states[:2], mats)
                    high = listed[3, steps + 1 if final else k]
                    phase = i if parts == 2 and not final else None
                    run_slots(listed[3, k - 1], high, listed, *states[:4], wide, half, width, phase)
                    if final:
                        store_flat(states[3], slots, made[0], width)
                    elif tied:
                        made[0][...] = jnp.zeros_like(made[0])

                state, made = call(
                    body,
                    piece_ins(pieces),
                    state,
                    closing,
                    width,
                    cut,
                    f"slots_step_{k}_{i}",
                    4,
                )
                token = made[0] if made else None
        back = swap(token)

        def last(given, states, made, mats, wide, half):
            listed = states[4]
            run_slots(listed[3, steps + 1], listed[3, steps], listed, *states[:4], wide, half, width)
            store_flat(states[3], 0, made[0], width)

        state, (own,) = call(last, [], state, [jax.ShapeDtypeStruct(flat.shape, F32)], width, 1, "slots_own", 2)
        result = own + back
    else:
        state = tables
        for k in range(1, steps + 1):
            for i in range(parts):
                send(k, i)
            pieces = (arrivals[0] if k == 1 else []) + arrivals[k]

            def body(given, states, made, mats, wide, half, pieces=pieces):
                fill(given[1:], pieces, given[0], states, mats)

            state, _ = call(body, [(meta, True)] + piece_ins(pieces), state, [], width, cut, f"table_step_{k}", 2)

        def group(given, states, made, mats, wide, half):
            meta_ref, names, rows = given
            result_ref, listed = made[:2]
            count = rows.shape[0]
            amp, acc = states[2:]
            total = order_slots([(names, 0)], meta_ref, chips, steps, listed)
            pad_order(listed, total, count)
            acc[...] = jnp.zeros_like(acc)
            load_matrices(rows, amp, 0, width)
            run_slots(0, listed[3, steps], listed, *states, wide, half, width)
            store_flat(acc, 0, result_ref, width)

        def grouped(rows, names):
            nonlocal state
            results = []
            for g in range(0, slots, GROUP):
                count = min(GROUP, slots - g)
                matrices = pltpu.VMEM(((count + 1) * pitch(width), LANE), F32)
                kept, made = call(
                    group,
                    [(meta, True), (names[g // keep : (g + count) // keep], True), (rows[g : g + count], False)],
                    [*state, matrices, matrices],
                    [
                        jax.ShapeDtypeStruct((count, cells), F32),
                        jax.ShapeDtypeStruct((5, count + max(UNROLL, steps + 2)), jnp.int32),
                    ],
                    width,
                    1,
                    f"slots_group_{g}",
                    20,
                )
                state = kept[:2]
                results.append(made[0])
            return jnp.concatenate(results) if len(results) > 1 else results[0]

        back = swap(grouped(swap(flat), swap(labels)))
        result = grouped(flat, labels) + back
    return result.reshape(pair_rows, keep, cells)


def solution(mesh):
    return jax.shard_map(
        functools.partial(shards, ring_order(mesh)),
        mesh=mesh,
        in_specs=(
            P(("groups", "pairs"), None, None),
            P(("groups", "pairs"), None),
            P(("groups", "pairs"), None),
        ),
        out_specs=P(("groups", "pairs"), None, None),
        check_vma=False,
    )
```

```python
import functools
import math

import jax
import jax.numpy as jnp
import numpy as np
from jax import lax
from jax.experimental import pallas as pl
from jax.experimental.pallas import tpu as pltpu
from jax.sharding import PartitionSpec as P

NB = 8
NAUX = 32
LANE = 128
UNROLL = 2
WIDTHS = (8, 4, 2)
PER = 8
GROUP = 64
BF = jnp.bfloat16
F32 = jnp.float32
NN = (((1,), (0,)), ((), ()))
VMEM_BYTES = 22 << 20
TOKEN = jax.ShapeDtypeStruct((8, LANE), F32)


def pitch(width):
    return width + 8 if width % 16 == 0 else width


def split(x):
    hi = x.astype(BF)
    return hi, (x - hi.astype(F32)).astype(BF)


def unpack(y0, y1, y2):
    lane = lax.broadcasted_iota(jnp.int32, y0.shape, 1)
    v1, v2 = jnp.where(lane >= 96, y0, y1), jnp.where(lane >= 64, y1, y2)
    return y0, pltpu.roll(v1, 32, 1), pltpu.roll(v2, 64, 1), pltpu.roll(y2, 96, 1)


def unflatten(read, write, width):
    for m in range(width // 4):
        for r, v in enumerate(unpack(*(read(3 * m + j) for j in range(3)))):
            write(4 * m + r, v)


def pack(v0, v1, v2, v3):
    lane = lax.broadcasted_iota(jnp.int32, v0.shape, 1)
    v1, v2, v3 = pltpu.roll(v1, 96, 1), pltpu.roll(v2, 64, 1), pltpu.roll(v3, 32, 1)
    return jnp.where(lane < 96, v0, v1), jnp.where(lane < 64, v1, v2), jnp.where(lane < 32, v2, v3)


def flatten(read, write, width):
    for m in range(width // 4):
        for j, y in enumerate(pack(*(read(4 * m + r) for r in range(4)))):
            write(3 * m + j, y)


def load_matrices(flat, mats, first, width):
    rows = flat.shape[0]
    step = min(8, rows)

    def group(g, carry):
        at = pl.multiple_of(g * step, step)
        base = pl.multiple_of((first + g * step) * pitch(width), 8)

        def read(j):
            return flat[pl.ds(at, step), j * LANE : (j + 1) * LANE]

        def write(e, v):
            mats[pl.ds(base + e, step, stride=pitch(width)), :] = v

        unflatten(read, write, width)
        return carry

    lax.fori_loop(0, rows // step, group, 0)


def store_flat(mats, first, out, width):
    rows = out.shape[0]
    step = min(8, rows)

    def group(g, carry):
        at = pl.multiple_of(g * step, step)
        base = pl.multiple_of((first + g * step) * pitch(width), 8)

        def read(e):
            return mats[pl.ds(base + e, step, stride=pitch(width)), :]

        def write(j, v):
            out[pl.ds(at, step), j * LANE : (j + 1) * LANE] = v

        flatten(read, write, width)
        return carry

    lax.fori_loop(0, rows // step, group, 0)


def fill_table(pieces, meta, tabs, mats, width, per_block):
    right, left = tabs
    for flat, offset, first, held in pieces:
        rows = flat.shape[0]
        load_matrices(flat, mats, 0, width)
        chip = meta[0, offset]
        block = chip // per_block
        lead = (chip % per_block) * held + first
        for i in range(0, rows, 4):
            four = [mats[(i + r) * pitch(width) : (i + r) * pitch(width) + width, :] for r in range(4)]
            blank = jnp.zeros((width, LANE - width), F32)
            turned = [jnp.concatenate([x.T[:width], blank], axis=1) for x in four]
            for table, matrices in ((left, four), (right, turned)):
                for j, y in enumerate(pack(*matrices)):
                    hi, lo = split(y)
                    at = pl.multiple_of(((lead + i) // 4 * 3 + j) * LANE, LANE)
                    table[block, 0:width, pl.ds(at, LANE)] = hi
                    table[block, width : 2 * width, pl.ds(at, LANE)] = lo


def order_slots(labels, meta, chips, steps, order):
    for r in range(steps + 2):
        order[3, r] = 0

    def ready_of(v):
        c, d = jnp.maximum(v, 0) >> 3, jnp.maximum(v, 0) & 7
        x, y = meta[0, chips + c], meta[0, chips + d]
        last = jnp.maximum(x, y)
        both = ((x >> 1) == (y >> 1)) & (x != y)
        ready = jnp.maximum((last >> 1) + jnp.where(both, 1, 0), 1)
        return jnp.where(v >= 0, ready, steps + 1), c, d, last & 1

    def tally(ref):
        for row in range(ref.shape[0]):

            def one(i, carry, row=row):
                ready = ready_of(ref[row, i])[0]
                order[3, ready] = order[3, ready] + 1
                return carry

            lax.fori_loop(0, ref.shape[1], one, 0, unroll=8)

    tally(labels[0][0])
    early = order[3, steps]
    for ref, _ in labels[1:]:
        tally(ref)
    early = jnp.maximum(early, order[3, steps] - early)
    total = 0
    for r in range(1, steps + 1):
        count = order[3, r]
        order[3, r] = total
        total = total + count
    order[3, steps + 1] = total
    early = early + order[3, steps]

    def put(ref, first):
        for row in range(ref.shape[0]):

            def one(i, carry, row=row):
                ready, c, d, part = ready_of(ref[row, i])
                n = order[3, ready]
                order[0, n] = first + row * ref.shape[1] + i
                order[1, n] = c
                order[2, n] = d
                order[4, n] = part
                order[3, ready] = n + 1
                return carry

            lax.fori_loop(0, ref.shape[1], one, 0, unroll=8)

    for ref, first in labels:
        put(ref, first)
    for r in range(1, steps):
        order[3, r] = order[3, r] // UNROLL
    order[3, 0] = 0
    order[3, steps] = (total + UNROLL - 1) // UNROLL
    order[3, steps + 1] = (early + UNROLL - 1) // UNROLL
    return total


def pad_order(order, total, dummy):
    for u in range(UNROLL - 1):
        order[0, total + u] = dummy
        order[1, total + u] = 0
        order[2, total + u] = 0
        order[4, total + u] = 0


def run_slots(low, high, order, right, left, amp, acc, wide, half, width, phase=None):
    cols = right.shape[2] // width
    if phase is not None:
        cols = cols // 2

    def some(base, count):
        ids = [tuple(order[k, base + u] for k in range(3)) for u in range(count)]
        starts = [0] * count
        if phase is not None:
            parts = [order[4, base + u] for u in range(count)]
            starts = [pl.multiple_of((p if phase == 0 else 1 - p) * (cols * width), LANE) for p in parts]
        for u, (s, _, _) in enumerate(ids):
            hi, lo = split(amp[pl.ds(pl.multiple_of(s * pitch(width), 8), width), 0:width])
            for at in (0, width):
                wide[u, 0:width, at : at + width] = hi
                wide[u, width : 2 * width, at : at + width] = lo
        for g in range(0, cols, PER):
            for u, (_, _, d) in enumerate(ids):
                span = pl.ds(starts[u] + g * width, PER * width)
                r = lax.dot_general(wide[u], right[d, :, span], NN, preferred_element_type=F32)
                r = r[:width] + r[width:]
                for j in range(0, PER, 4):
                    at = [(j // 4 * 3 + k) * LANE for k in range(4)]
                    for q, v in enumerate(unpack(*(r[:, at[k] : at[k + 1]] for k in range(3)))):
                        hi, lo = split(v)
                        p = g + j + q
                        half[u, p * width : (p + 1) * width, 0:LANE] = hi
                        half[u, p * width : (p + 1) * width, LANE : 2 * LANE] = lo
        for u, (s, c, _) in enumerate(ids):
            span = pl.ds(starts[u], cols * width)
            o = lax.dot_general(left[c, :, span], half[u, 0 : cols * width, :], NN, preferred_element_type=F32)
            o = o[:width, :LANE] + o[width:, :LANE] + o[:width, LANE:]
            at = pl.ds(pl.multiple_of(s * pitch(width), 8), width)
            acc[at, :] = acc[at, :] + o if phase == 1 else o

    done = low * UNROLL
    left_over = (high - low) * UNROLL
    for count in WIDTHS:
        turns = left_over // count

        def turn(i, carry, done=done, count=count):
            some(done + i * count, count)
            return carry

        lax.fori_loop(0, turns, turn, 0)
        done = done + turns * count
        left_over = left_over - turns * count


def scratch(cols, width, rows):
    return [
        pltpu.VMEM((max(rows, 1) * pitch(width), LANE), F32),
        pltpu.VMEM((WIDTHS[0], 2 * width, 2 * width), BF),
        pltpu.VMEM((WIDTHS[0], cols * width, 2 * LANE), BF),
    ]


def resident(x):
    return pltpu.with_memory_space_constraint(x, pltpu.SMEM if x.dtype == jnp.int32 else pltpu.VMEM)


def call(body, ins, keep, outs, width, rows, name, micros):
    vm, sm = pl.BlockSpec(memory_space=pltpu.VMEM), pl.BlockSpec(memory_space=pltpu.SMEM)
    arrays = [x for x, _ in ins]
    specs = [sm if scalars else vm for _, scalars in ins]
    shapes, aliases, olds = [], {}, 0
    for i, x in enumerate(keep):
        if isinstance(x, jax.Array):
            aliases[len(arrays)] = i
            arrays.append(resident(x))
            specs.append(sm if x.dtype == jnp.int32 else vm)
            olds += 1
            shapes.append((pltpu.SMEM if x.dtype == jnp.int32 else pltpu.VMEM)(x.shape, x.dtype))
        else:
            shapes.append(x)
    specs_out = [sm if x.dtype == jnp.int32 else vm for x in [*keep, *outs]]

    def kernel(*refs):
        refs = list(refs)
        given, refs = refs[: len(ins)], refs[len(ins) + olds :]
        states, refs = refs[: len(keep)], refs[len(keep) :]
        made, refs = refs[: len(outs)], refs[len(outs) :]
        body(given, states, made, *refs)

    results = pl.pallas_call(
        kernel,
        out_shape=shapes + list(outs),
        in_specs=specs,
        out_specs=specs_out,
        input_output_aliases=aliases,
        scratch_shapes=scratch(NAUX // 2, width, rows),
        compiler_params=pltpu.CompilerParams(vmem_limit_bytes=VMEM_BYTES),
        cost_estimate=pl.CostEstimate(flops=int(micros * 1e9), bytes_accessed=int(micros * 3e6), transcendentals=0),
        name=name,
    )(*arrays)
    return results[: len(keep)], results[len(keep) :]


def after(arrays, token):
    anywhere = pl.BlockSpec(memory_space=pl.ANY)
    return pl.pallas_call(
        lambda *refs: None,
        out_shape=[jax.ShapeDtypeStruct(x.shape, x.dtype) for x in arrays],
        in_specs=[anywhere] * (len(arrays) + 1),
        out_specs=[anywhere] * len(arrays),
        input_output_aliases={i: i for i in range(len(arrays))},
        compiler_params=pltpu.CompilerParams(vmem_limit_bytes=1 << 20),
        name="gate",
    )(*arrays, token)


def copy_rows(x, parts, token):
    rows = x.shape[0] // parts

    def kernel(whole, _, *refs):
        outs, sems = refs[:parts], refs[parts]
        copies = [
            pltpu.make_async_copy(whole.at[pl.ds(i * rows, rows)], outs[i], sems.at[i]) for i in range(parts)
        ]
        for c in copies:
            c.start()
        for c in copies:
            c.wait()

    return pl.pallas_call(
        kernel,
        out_shape=[pltpu.VMEM((rows, x.shape[1]), x.dtype)] * parts,
        in_specs=[pl.BlockSpec(memory_space=pl.ANY)] * 2,
        out_specs=[pl.BlockSpec(memory_space=pltpu.VMEM)] * parts,
        scratch_shapes=[pltpu.SemaphoreType.DMA((parts,))],
        compiler_params=pltpu.CompilerParams(vmem_limit_bytes=1 << 20),
        name="copy_rows",
    )(x, token)


def ring_order(mesh):
    devices = mesh.devices.reshape(mesh.shape["groups"], mesh.shape["pairs"])[0, ::2]
    count = len(devices)
    places = [tuple(getattr(d, "coords", None) or (i, 0, 0)) for i, d in enumerate(devices)]
    spread = [sorted({p[a] for p in places}) for a in range(len(places[0]))]
    varying = [a for a in range(len(spread)) if len(spread[a]) > 1]
    if len(varying) == 2 and min(len(spread[a]) for a in varying) == 2:
        short, long = sorted(varying, key=lambda a: len(spread[a]))
        up = sorted((i for i in range(count) if places[i][short] == spread[short][0]), key=lambda i: places[i][long])
        down = sorted((i for i in range(count) if places[i][short] != spread[short][0]), key=lambda i: -places[i][long])
        return up + down
    return list(range(count))


def shards(ring, amplitudes, block_list, factors):
    pair_rows, keep, cells = amplitudes.shape
    width = math.isqrt(cells)
    slots = pair_rows * keep
    held = factors.shape[0]
    chips = len(ring)
    steps = chips // 2
    per_block = NAUX // (2 * held)
    parts = 2 if per_block == 1 else 1
    cut = held // parts

    place = {c: i for i, c in enumerate(ring)}
    table = np.zeros((chips, chips + NB), np.int32)
    for c in range(chips):
        for j in range(chips):
            table[c, j] = ring[(place[c] + j) % chips]
        for j in range(chips):
            far = min(j, chips - j)
            b = table[c, j] // per_block
            table[c, chips + b] = max(table[c, chips + b], 2 * far + (0 < j < chips - j))

    def shift(x, by):
        pairs = [
            (2 * ring[i] + core, 2 * ring[(i + by) % chips] + core) for i in range(chips) for core in range(2)
        ]
        return lax.ppermute(x, "pairs", pairs)

    def swap(x):
        return lax.ppermute(x, "pairs", [(i, i ^ 1) for i in range(2 * chips)])

    flat = amplitudes.reshape(slots, cells)
    labels = block_list
    row = lax.axis_index("pairs") // 2
    meta = lax.dynamic_slice(jnp.asarray(table), (row, 0), (1, chips + NB))

    up = [factors[i * cut : (i + 1) * cut] for i in range(parts)]
    down = list(up)
    arrivals = [[(x, 0, h * cut) for h, x in enumerate(up)]]
    cols = NAUX // 2
    tables = [pltpu.VMEM((NB, 2 * width, cols * width), BF)] * 2

    def fill(refs, pieces, meta_ref, tabs, mats):
        fill_table([(ref, o, f, held) for ref, (_, o, f) in zip(refs, pieces)], meta_ref, tabs, mats, width, per_block)

    def piece_ins(pieces):
        return [(x, False) for x, _, _ in pieces]

    def send(k, i):
        if len(arrivals) == k:
            arrivals.append([])
        o = parts - 1 - i
        if k < steps or i == 0:
            up[i] = shift(up[i], 1)
            arrivals[k].append((up[i], chips - k, i * cut))
        if k < steps or (i == 0 and parts == 2):
            down[o] = shift(down[o], -1)
            arrivals[k].append((down[o], k, o * cut))

    if 2 * slots <= GROUP:
        matrices = pltpu.VMEM(((2 * slots + 1) * pitch(width), LANE), F32)
        listed_shape = pltpu.SMEM((6, max(2 * slots + UNROLL, chips + NB)), jnp.int32)
        other_flat, other_labels = swap(flat), swap(labels)
        send(1, 0)
        if parts == 2:
            down[0], up[1] = copy_rows(factors, parts, other_labels)
            send(1, 1)

        def arrange(given, states, made, mats, wide, half):
            meta_ref, own_l, other_l = given
            (listed,) = states
            total = order_slots([(other_l, slots), (own_l, 0)], meta_ref, chips, steps, listed)
            pad_order(listed, total, 2 * slots)
            for i in range(chips + NB):
                listed[5, i] = meta_ref[0, i]

        (listed,), _ = call(
            arrange, [(meta, True), (labels, True), (other_labels, True)], [listed_shape], [], width, 1, "arrange", 2
        )

        def prepare(given, states, made, mats, wide, half):
            load_matrices(given[0], states[2], 0, width)
            load_matrices(given[1], states[2], slots, width)
            states[3][...] = jnp.zeros_like(states[3])
            made[0][...] = jnp.zeros_like(made[0])
            fill(given[2:], arrivals[0], states[4].at[pl.ds(5, 1)], states[:2], mats)

        state, (token,) = call(
            prepare,
            [(flat, False), (other_flat, False)] + piece_ins(arrivals[0]),
            tables + [matrices, matrices, listed],
            [TOKEN],
            width,
            cut,
            "prepare",
            4,
        )

        for k in range(1, steps + 1):
            final = k == steps
            for i in range(1 if final else parts):
                o = parts - 1 - i
                pieces = arrivals[k]
                if not final:
                    if k < steps - 1 or i == 0:
                        up[i], down[o] = after([up[i], down[o]], token)
                    pieces = [(up[i], chips - k, i * cut), (down[o], k, o * cut)]
                    send(k + 1, i)
                tied = k < steps - 1
                closing = [jax.ShapeDtypeStruct(flat.shape, F32)] if final else [TOKEN] * tied

                def body(given, states, made, mats, wide, half, k=k, i=i, pieces=pieces, final=final, tied=tied):
                    listed = states[4]
                    fill(given, pieces, listed.at[pl.ds(5, 1)], states[:2], mats)
                    high = listed[3, steps + 1 if final else k]
                    phase = i if parts == 2 and not final else None
                    run_slots(listed[3, k - 1], high, listed, *states[:4], wide, half, width, phase)
                    if final:
                        store_flat(states[3], slots, made[0], width)
                    elif tied:
                        made[0][...] = jnp.zeros_like(made[0])

                state, made = call(
                    body,
                    piece_ins(pieces),
                    state,
                    closing,
                    width,
                    cut,
                    f"slots_step_{k}_{i}",
                    4,
                )
                token = made[0] if made else None
        back = swap(token)

        def last(given, states, made, mats, wide, half):
            listed = states[4]
            run_slots(listed[3, steps + 1], listed[3, steps], listed, *states[:4], wide, half, width)
            store_flat(states[3], 0, made[0], width)

        state, (own,) = call(last, [], state, [jax.ShapeDtypeStruct(flat.shape, F32)], width, 1, "slots_own", 2)
        result = own + back
    else:
        state = tables
        for k in range(1, steps + 1):
            for i in range(parts):
                send(k, i)
            pieces = (arrivals[0] if k == 1 else []) + arrivals[k]

            def body(given, states, made, mats, wide, half, pieces=pieces):
                fill(given[1:], pieces, given[0], states, mats)

            state, _ = call(body, [(meta, True)] + piece_ins(pieces), state, [], width, cut, f"table_step_{k}", 2)

        def group(given, states, made, mats, wide, half):
            meta_ref, names, rows = given
            result_ref, listed = made[:2]
            count = rows.shape[0]
            amp, acc = states[2:]
            total = order_slots([(names, 0)], meta_ref, chips, steps, listed)
            pad_order(listed, total, count)
            acc[...] = jnp.zeros_like(acc)
            load_matrices(rows, amp, 0, width)
            run_slots(0, listed[3, steps], listed, *states, wide, half, width)
            store_flat(acc, 0, result_ref, width)

        def grouped(rows, names):
            nonlocal state
            results = []
            for g in range(0, slots, GROUP):
                count = min(GROUP, slots - g)
                matrices = pltpu.VMEM(((count + 1) * pitch(width), LANE), F32)
                kept, made = call(
                    group,
                    [(meta, True), (names[g // keep : (g + count) // keep], True), (rows[g : g + count], False)],
                    [*state, matrices, matrices],
                    [
                        jax.ShapeDtypeStruct((count, cells), F32),
                        jax.ShapeDtypeStruct((5, count + max(UNROLL, steps + 2)), jnp.int32),
                    ],
                    width,
                    1,
                    f"slots_group_{g}",
                    20,
                )
                state = kept[:2]
                results.append(made[0])
            return jnp.concatenate(results) if len(results) > 1 else results[0]

        back = swap(grouped(swap(flat), swap(labels)))
        result = grouped(flat, labels) + back
    return result.reshape(pair_rows, keep, cells)


def solution(mesh):
    return jax.shard_map(
        functools.partial(shards, ring_order(mesh)),
        mesh=mesh,
        in_specs=(
            P(("groups", "pairs"), None, None),
            P(("groups", "pairs"), None),
            P(("groups", "pairs"), None),
        ),
        out_specs=P(("groups", "pairs"), None, None),
        check_vma=False,
    )
```

```python
import functools
import math

import jax
import jax.numpy as jnp
import numpy as np
from jax import lax
from jax.experimental import pallas as pl
from jax.experimental.pallas import tpu as pltpu
from jax.sharding import PartitionSpec as P

NB = 8
NAUX = 32
LANE = 128
UNROLL = 2
WIDTHS = (8, 4, 2)
PER = 8
GROUP = 64
BF = jnp.bfloat16
F32 = jnp.float32
NN = (((1,), (0,)), ((), ()))
VMEM_BYTES = 22 << 20
TOKEN = jax.ShapeDtypeStruct((8, LANE), F32)


def pitch(width):
    return width + 8 if width % 16 == 0 else width


def split(x):
    hi = x.astype(BF)
    return hi, (x - hi.astype(F32)).astype(BF)


def unpack(y0, y1, y2):
    lane = lax.broadcasted_iota(jnp.int32, y0.shape, 1)
    v1, v2 = jnp.where(lane >= 96, y0, y1), jnp.where(lane >= 64, y1, y2)
    return y0, pltpu.roll(v1, 32, 1), pltpu.roll(v2, 64, 1), pltpu.roll(y2, 96, 1)


def unflatten(read, write, width):
    for m in range(width // 4):
        for r, v in enumerate(unpack(*(read(3 * m + j) for j in range(3)))):
            write(4 * m + r, v)


def pack(v0, v1, v2, v3):
    lane = lax.broadcasted_iota(jnp.int32, v0.shape, 1)
    v1, v2, v3 = pltpu.roll(v1, 96, 1), pltpu.roll(v2, 64, 1), pltpu.roll(v3, 32, 1)
    return jnp.where(lane < 96, v0, v1), jnp.where(lane < 64, v1, v2), jnp.where(lane < 32, v2, v3)


def flatten(read, write, width):
    for m in range(width // 4):
        for j, y in enumerate(pack(*(read(4 * m + r) for r in range(4)))):
            write(3 * m + j, y)


def load_matrices(flat, mats, first, width):
    rows = flat.shape[0]
    step = min(8, rows)

    def group(g, carry):
        at = pl.multiple_of(g * step, step)
        base = pl.multiple_of((first + g * step) * pitch(width), 8)

        def read(j):
            return flat[pl.ds(at, step), j * LANE : (j + 1) * LANE]

        def write(e, v):
            mats[pl.ds(base + e, step, stride=pitch(width)), :] = v

        unflatten(read, write, width)
        return carry

    lax.fori_loop(0, rows // step, group, 0)


def store_flat(mats, first, out, width):
    rows = out.shape[0]
    step = min(8, rows)

    def group(g, carry):
        at = pl.multiple_of(g * step, step)
        base = pl.multiple_of((first + g * step) * pitch(width), 8)

        def read(e):
            return mats[pl.ds(base + e, step, stride=pitch(width)), :]

        def write(j, v):
            out[pl.ds(at, step), j * LANE : (j + 1) * LANE] = v

        flatten(read, write, width)
        return carry

    lax.fori_loop(0, rows // step, group, 0)


def fill_table(pieces, meta, tabs, mats, width, per_block):
    right, left = tabs
    for flat, offset, first, held in pieces:
        rows = flat.shape[0]
        load_matrices(flat, mats, 0, width)
        chip = meta[0, offset]
        block = chip // per_block
        lead = (chip % per_block) * held + first
        for i in range(0, rows, 4):
            four = [mats[(i + r) * pitch(width) : (i + r) * pitch(width) + width, :] for r in range(4)]
            blank = jnp.zeros((width, LANE - width), F32)
            turned = [jnp.concatenate([x.T[:width], blank], axis=1) for x in four]
            for table, matrices in ((left, four), (right, turned)):
                for j, y in enumerate(pack(*matrices)):
                    hi, lo = split(y)
                    at = pl.multiple_of(((lead + i) // 4 * 3 + j) * LANE, LANE)
                    table[block, 0:width, pl.ds(at, LANE)] = hi
                    table[block, width : 2 * width, pl.ds(at, LANE)] = lo


def order_slots(labels, meta, chips, steps, order):
    for r in range(steps + 2):
        order[3, r] = 0

    def ready_of(v):
        c, d = jnp.maximum(v, 0) >> 3, jnp.maximum(v, 0) & 7
        x, y = meta[0, chips + c], meta[0, chips + d]
        last = jnp.maximum(x, y)
        both = ((x >> 1) == (y >> 1)) & (x != y)
        ready = jnp.maximum((last >> 1) + jnp.where(both, 1, 0), 1)
        return jnp.where(v >= 0, ready, steps + 1), c, d, last & 1

    def tally(ref):
        for row in range(ref.shape[0]):

            def one(i, carry, row=row):
                ready = ready_of(ref[row, i])[0]
                order[3, ready] = order[3, ready] + 1
                return carry

            lax.fori_loop(0, ref.shape[1], one, 0, unroll=8)

    tally(labels[0][0])
    early = order[3, steps]
    for ref, _ in labels[1:]:
        tally(ref)
    early = jnp.maximum(early, order[3, steps] - early)
    total = 0
    for r in range(1, steps + 1):
        count = order[3, r]
        order[3, r] = total
        total = total + count
    order[3, steps + 1] = total
    early = early + order[3, steps]

    def put(ref, first):
        for row in range(ref.shape[0]):

            def one(i, carry, row=row):
                ready, c, d, part = ready_of(ref[row, i])
                n = order[3, ready]
                order[0, n] = first + row * ref.shape[1] + i
                order[1, n] = c
                order[2, n] = d
                order[4, n] = part
                order[3, ready] = n + 1
                return carry

            lax.fori_loop(0, ref.shape[1], one, 0, unroll=8)

    for ref, first in labels:
        put(ref, first)
    for r in range(1, steps):
        order[3, r] = order[3, r] // UNROLL
    order[3, 0] = 0
    order[3, steps] = (total + UNROLL - 1) // UNROLL
    order[3, steps + 1] = (early + UNROLL - 1) // UNROLL
    return total


def pad_order(order, total, dummy):
    for u in range(UNROLL - 1):
        order[0, total + u] = dummy
        order[1, total + u] = 0
        order[2, total + u] = 0
        order[4, total + u] = 0


def run_slots(low, high, order, right, left, amp, acc, wide, half, width, phase=None):
    cols = right.shape[2] // width
    if phase is not None:
        cols = cols // 2

    def some(base, count):
        ids = [tuple(order[k, base + u] for k in range(3)) for u in range(count)]
        starts = [0] * count
        if phase is not None:
            parts = [order[4, base + u] for u in range(count)]
            starts = [pl.multiple_of((p if phase == 0 else 1 - p) * (cols * width), LANE) for p in parts]
        for u, (s, _, _) in enumerate(ids):
            hi, lo = split(amp[pl.ds(pl.multiple_of(s * pitch(width), 8), width), 0:width])
            for at in (0, width):
                wide[u, 0:width, at : at + width] = hi
                wide[u, width : 2 * width, at : at + width] = lo
        for g in range(0, cols, PER):
            for u, (_, _, d) in enumerate(ids):
                span = pl.ds(starts[u] + g * width, PER * width)
                r = lax.dot_general(wide[u], right[d, :, span], NN, preferred_element_type=F32)
                r = r[:width] + r[width:]
                for j in range(0, PER, 4):
                    at = [(j // 4 * 3 + k) * LANE for k in range(4)]
                    for q, v in enumerate(unpack(*(r[:, at[k] : at[k + 1]] for k in range(3)))):
                        hi, lo = split(v)
                        p = g + j + q
                        half[u, p * width : (p + 1) * width, 0:LANE] = hi
                        half[u, p * width : (p + 1) * width, LANE : 2 * LANE] = lo
        for u, (s, c, _) in enumerate(ids):
            span = pl.ds(starts[u], cols * width)
            o = lax.dot_general(left[c, :, span], half[u, 0 : cols * width, :], NN, preferred_element_type=F32)
            o = o[:width, :LANE] + o[width:, :LANE] + o[:width, LANE:]
            at = pl.ds(pl.multiple_of(s * pitch(width), 8), width)
            acc[at, :] = acc[at, :] + o if phase == 1 else o

    done = low * UNROLL
    left_over = (high - low) * UNROLL
    for count in WIDTHS:
        turns = left_over // count

        def turn(i, carry, done=done, count=count):
            some(done + i * count, count)
            return carry

        lax.fori_loop(0, turns, turn, 0)
        done = done + turns * count
        left_over = left_over - turns * count


def scratch(cols, width, rows):
    return [
        pltpu.VMEM(((rows + 1) * pitch(width), LANE), F32),
        pltpu.VMEM((WIDTHS[0], 2 * width, 2 * width), BF),
        pltpu.VMEM((WIDTHS[0], cols * width, 2 * LANE), BF),
    ]


def resident(x):
    return pltpu.with_memory_space_constraint(x, pltpu.SMEM if x.dtype == jnp.int32 else pltpu.VMEM)


def call(body, ins, keep, outs, width, rows, name, micros):
    vm, sm = pl.BlockSpec(memory_space=pltpu.VMEM), pl.BlockSpec(memory_space=pltpu.SMEM)
    arrays = [x for x, _ in ins]
    specs = [sm if scalars else vm for _, scalars in ins]
    shapes, aliases, olds = [], {}, 0
    for i, x in enumerate(keep):
        if isinstance(x, jax.Array):
            aliases[len(arrays)] = i
            arrays.append(resident(x))
            specs.append(sm if x.dtype == jnp.int32 else vm)
            olds += 1
            shapes.append((pltpu.SMEM if x.dtype == jnp.int32 else pltpu.VMEM)(x.shape, x.dtype))
        else:
            shapes.append(x)
    specs_out = [sm if x.dtype == jnp.int32 else vm for x in [*keep, *outs]]

    def kernel(*refs):
        refs = list(refs)
        given, refs = refs[: len(ins)], refs[len(ins) + olds :]
        states, refs = refs[: len(keep)], refs[len(keep) :]
        made, refs = refs[: len(outs)], refs[len(outs) :]
        body(given, states, made, *refs)

    results = pl.pallas_call(
        kernel,
        out_shape=shapes + list(outs),
        in_specs=specs,
        out_specs=specs_out,
        input_output_aliases=aliases,
        scratch_shapes=scratch(NAUX // 2, width, rows),
        compiler_params=pltpu.CompilerParams(vmem_limit_bytes=VMEM_BYTES),
        cost_estimate=pl.CostEstimate(flops=int(micros * 1e9), bytes_accessed=int(micros * 3e6), transcendentals=0),
        name=name,
    )(*arrays)
    return results[: len(keep)], results[len(keep) :]


def after(arrays, token):
    anywhere = pl.BlockSpec(memory_space=pl.ANY)
    return pl.pallas_call(
        lambda *refs: None,
        out_shape=[jax.ShapeDtypeStruct(x.shape, x.dtype) for x in arrays],
        in_specs=[anywhere] * (len(arrays) + 1),
        out_specs=[anywhere] * len(arrays),
        input_output_aliases={i: i for i in range(len(arrays))},
        compiler_params=pltpu.CompilerParams(vmem_limit_bytes=1 << 20),
        name="gate",
    )(*arrays, token)


def copy_rows(x, parts, token):
    rows = x.shape[0] // parts

    def kernel(whole, _, *refs):
        outs, sems = refs[:parts], refs[parts]
        copies = [
            pltpu.make_async_copy(whole.at[pl.ds(i * rows, rows)], outs[i], sems.at[i]) for i in range(parts)
        ]
        for c in copies:
            c.start()
        for c in copies:
            c.wait()

    return pl.pallas_call(
        kernel,
        out_shape=[pltpu.VMEM((rows, x.shape[1]), x.dtype)] * parts,
        in_specs=[pl.BlockSpec(memory_space=pl.ANY)] * 2,
        out_specs=[pl.BlockSpec(memory_space=pltpu.VMEM)] * parts,
        scratch_shapes=[pltpu.SemaphoreType.DMA((parts,))],
        compiler_params=pltpu.CompilerParams(vmem_limit_bytes=1 << 20),
        name="copy_rows",
    )(x, token)


def ring_order(mesh):
    devices = mesh.devices.reshape(mesh.shape["groups"], mesh.shape["pairs"])[0, ::2]
    count = len(devices)
    places = [tuple(getattr(d, "coords", None) or (i, 0, 0)) for i, d in enumerate(devices)]
    spread = [sorted({p[a] for p in places}) for a in range(len(places[0]))]
    varying = [a for a in range(len(spread)) if len(spread[a]) > 1]
    if len(varying) == 2 and min(len(spread[a]) for a in varying) == 2:
        short, long = sorted(varying, key=lambda a: len(spread[a]))
        up = sorted((i for i in range(count) if places[i][short] == spread[short][0]), key=lambda i: places[i][long])
        down = sorted((i for i in range(count) if places[i][short] != spread[short][0]), key=lambda i: -places[i][long])
        return up + down
    return list(range(count))


def shards(ring, amplitudes, block_list, factors):
    pair_rows, keep, cells = amplitudes.shape
    width = math.isqrt(cells)
    slots = pair_rows * keep
    held = factors.shape[0]
    chips = len(ring)
    steps = chips // 2
    per_block = NAUX // (2 * held)
    parts = 2 if per_block == 1 else 1
    cut = held // parts

    place = {c: i for i, c in enumerate(ring)}
    table = np.zeros((chips, chips + NB), np.int32)
    for c in range(chips):
        for j in range(chips):
            table[c, j] = ring[(place[c] + j) % chips]
        for j in range(chips):
            far = min(j, chips - j)
            b = table[c, j] // per_block
            table[c, chips + b] = max(table[c, chips + b], 2 * far + (0 < j < chips - j))

    def shift(x, by):
        pairs = [
            (2 * ring[i] + core, 2 * ring[(i + by) % chips] + core) for i in range(chips) for core in range(2)
        ]
        return lax.ppermute(x, "pairs", pairs)

    def swap(x):
        return lax.ppermute(x, "pairs", [(i, i ^ 1) for i in range(2 * chips)])

    flat = amplitudes.reshape(slots, cells)
    labels = block_list
    row = lax.axis_index("pairs") // 2
    meta = lax.dynamic_slice(jnp.asarray(table), (row, 0), (1, chips + NB))

    up = [factors[i * cut : (i + 1) * cut] for i in range(parts)]
    down = list(up)
    arrivals = [[(x, 0, h * cut) for h, x in enumerate(up)]]
    cols = NAUX // 2
    tables = [pltpu.VMEM((NB, 2 * width, cols * width), BF)] * 2

    def fill(refs, pieces, meta_ref, tabs, mats):
        fill_table([(ref, o, f, held) for ref, (_, o, f) in zip(refs, pieces)], meta_ref, tabs, mats, width, per_block)

    def piece_ins(pieces):
        return [(x, False) for x, _, _ in pieces]

    def send(k, i):
        if len(arrivals) == k:
            arrivals.append([])
        o = parts - 1 - i
        if k < steps or i == 0:
            up[i] = shift(up[i], 1)
            arrivals[k].append((up[i], chips - k, i * cut))
        if k < steps or (i == 0 and parts == 2):
            down[o] = shift(down[o], -1)
            arrivals[k].append((down[o], k, o * cut))

    if 2 * slots <= GROUP:
        matrices = pltpu.VMEM(((2 * slots + 1) * pitch(width), LANE), F32)
        listed_shape = pltpu.SMEM((6, max(2 * slots + UNROLL, chips + NB)), jnp.int32)
        other_flat, other_labels = swap(flat), swap(labels)
        send(1, 0)
        if parts == 2:
            down[0], up[1] = copy_rows(factors, parts, other_labels)
            send(1, 1)

        def arrange(given, states, made, mats, wide, half):
            meta_ref, own_l, other_l = given
            (listed,) = states
            total = order_slots([(other_l, slots), (own_l, 0)], meta_ref, chips, steps, listed)
            pad_order(listed, total, 2 * slots)
            for i in range(chips + NB):
                listed[5, i] = meta_ref[0, i]

        (listed,), _ = call(
            arrange, [(meta, True), (labels, True), (other_labels, True)], [listed_shape], [], width, 1, "arrange", 2
        )

        def prepare(given, states, made, mats, wide, half):
            load_matrices(given[0], states[2], 0, width)
            load_matrices(given[1], states[2], slots, width)
            states[3][...] = jnp.zeros_like(states[3])
            made[0][...] = jnp.zeros_like(made[0])
            fill(given[2:], arrivals[0], states[4].at[pl.ds(5, 1)], states[:2], mats)

        state, (token,) = call(
            prepare,
            [(flat, False), (other_flat, False)] + piece_ins(arrivals[0]),
            tables + [matrices, matrices, listed],
            [TOKEN],
            width,
            cut,
            "prepare",
            4,
        )

        for k in range(1, steps + 1):
            final = k == steps
            for i in range(1 if final else parts):
                o = parts - 1 - i
                pieces = arrivals[k]
                if not final:
                    if k < steps - 1 or i == 0:
                        up[i], down[o] = after([up[i], down[o]], token)
                    pieces = [(up[i], chips - k, i * cut), (down[o], k, o * cut)]
                    send(k + 1, i)
                tied = k < steps - 1
                closing = [jax.ShapeDtypeStruct(flat.shape, F32)] if final else [TOKEN] * tied

                def body(given, states, made, mats, wide, half, k=k, i=i, pieces=pieces, final=final, tied=tied):
                    listed = states[4]
                    fill(given, pieces, listed.at[pl.ds(5, 1)], states[:2], mats)
                    high = listed[3, steps + 1 if final else k]
                    phase = i if parts == 2 and not final else None
                    run_slots(listed[3, k - 1], high, listed, *states[:4], wide, half, width, phase)
                    if final:
                        store_flat(states[3], slots, made[0], width)
                    elif tied:
                        made[0][...] = jnp.zeros_like(made[0])

                state, made = call(
                    body,
                    piece_ins(pieces),
                    state,
                    closing,
                    width,
                    cut,
                    f"slots_step_{k}_{i}",
                    4,
                )
                token = made[0] if made else None
        back = swap(token)

        def last(given, states, made, mats, wide, half):
            listed = states[4]
            run_slots(listed[3, steps + 1], listed[3, steps], listed, *states[:4], wide, half, width)
            store_flat(states[3], 0, made[0], width)

        state, (own,) = call(last, [], state, [jax.ShapeDtypeStruct(flat.shape, F32)], width, 1, "slots_own", 2)
        result = own + back
    else:
        state = tables
        for k in range(1, steps + 1):
            for i in range(parts):
                send(k, i)
            pieces = (arrivals[0] if k == 1 else []) + arrivals[k]

            def body(given, states, made, mats, wide, half, pieces=pieces):
                fill(given[1:], pieces, given[0], states, mats)

            state, _ = call(body, [(meta, True)] + piece_ins(pieces), state, [], width, cut, f"table_step_{k}", 2)

        def group(given, states, made, mats, wide, half):
            meta_ref, names, rows = given
            result_ref, listed = made[:2]
            count = rows.shape[0]
            amp, acc = states[2:]
            total = order_slots([(names, 0)], meta_ref, chips, steps, listed)
            pad_order(listed, total, count)
            acc[...] = jnp.zeros_like(acc)
            load_matrices(rows, amp, 0, width)
            run_slots(0, listed[3, steps], listed, *states, wide, half, width)
            store_flat(acc, 0, result_ref, width)

        def grouped(rows, names):
            nonlocal state
            results = []
            for g in range(0, slots, GROUP):
                count = min(GROUP, slots - g)
                matrices = pltpu.VMEM(((count + 1) * pitch(width), LANE), F32)
                kept, made = call(
                    group,
                    [(meta, True), (names[g // keep : (g + count) // keep], True), (rows[g : g + count], False)],
                    [*state, matrices, matrices],
                    [
                        jax.ShapeDtypeStruct((count, cells), F32),
                        jax.ShapeDtypeStruct((5, count + max(UNROLL, steps + 2)), jnp.int32),
                    ],
                    width,
                    1,
                    f"slots_group_{g}",
                    20,
                )
                state = kept[:2]
                results.append(made[0])
            return jnp.concatenate(results) if len(results) > 1 else results[0]

        back = swap(grouped(swap(flat), swap(labels)))
        result = grouped(flat, labels) + back
    return result.reshape(pair_rows, keep, cells)


def solution(mesh):
    return jax.shard_map(
        functools.partial(shards, ring_order(mesh)),
        mesh=mesh,
        in_specs=(
            P(("groups", "pairs"), None, None),
            P(("groups", "pairs"), None),
            P(("groups", "pairs"), None),
        ),
        out_specs=P(("groups", "pairs"), None, None),
        check_vma=False,
    )
```
